512 devices in a mesh: sec: 2 (over core), seq: 32 (over y, x), mp: 8 (over z).
Axes of the slice: x: 4, y: 8, z: 8, core: 2. Of those that a mesh axis runs over, the one named last changes fastest.
Arguments:
- hidden: bfloat16 [2, 4608, 8192], P(None, 'seq'), may hold values from -6 to 6
- norm_gain: float32 [2, 8192], P('sec'), may hold values from 0.1 to 1.9
- query_weight: bfloat16 [2, 8192, 4096], P('sec', 'seq', 'mp'), may hold values from -0.0625 to 0.0625
- keyvalue_weight: bfloat16 [2, 8192, 2, 1024], P('sec', 'seq', None, 'mp'), may hold values from -0.0625 to 0.0625
- policy_head: float32 [4096], P('mp'), may hold values from -0.3125 to 0.3125
- critic_heads: float32 [2, 4096], P(None, 'mp'), may hold values from -0.3125 to 0.3125
- lengths: int32 [2, 64], replicated, may hold values from 1 to 576, 4608 in all within a row
Outputs:
- policy_scores: float32 [2, 4608], P(None, 'seq')
- advantages: float32 [2, 4608], P(None, 'seq')
- returns: float32 [2, 4608], P(None, 'seq')
The draws below stay inside these ranges and needn't reach their ends.
Inputs may be any that keep to these rules, and one draw needn't show every extreme that they name: Each micro-batch's lengths sum to 4608; in each micro-batch one length is exactly 576.
All inputs are finite; a program needn't handle non-finite values.
Results may differ from the reference program's by a relative error of at most 0.0071.
Values may be sent and summed in bfloat16 or wider, within the bound.
A program may use at most 128 MiB of HBM per device.

```python
import math
import jax
import jax.numpy as jnp
import numpy as np
from jax import lax

D = 8192
HEAD_DIM = 128
KV_HEADS = 8
HEADS = 32
ROWS = 144
MICRO = 2
REACH = 4
LMAX = 576
TOKENS = 4608
NRESP = 64


def levels(key, extent, shards, low, high):
    def one(dim, blocks):
        heights = jax.random.uniform(jax.random.fold_in(jax.random.fold_in(key, 6), dim), (blocks,), jnp.float32, low / len(shards), high / len(shards))
        return jnp.repeat(jnp.exp(heights), extent[dim] // blocks).reshape((-1,) + (1,) * (len(extent) - dim - 1))

    factor_of = one(*shards[0])
    for cut in shards[1:]:
        factor_of = factor_of * one(*cut)
    return factor_of


def length_profile(count, total, limit, slope):
    weights = [(1 << 20) // math.isqrt(grade ** slope) + 1 for grade in range(2, count + 1)]
    surplus, given = total - limit - (count - 1), [1] * (count - 1)
    while surplus > 0:
        candidates = [i for i in range(count - 1) if given[i] < limit]
        mass, remaining = sum([weights[i] for i in candidates]), surplus
        for i in candidates:
            extra = min(limit - given[i], max(1, remaining * weights[i] // mass), surplus)
            given[i] = given[i] + extra
            surplus = surplus - extra
    return np.array([limit] + given)


def uneven_parts(own_key, number_of, total, most, slope):
    if number_of == 2:
        one = jax.random.randint(own_key, (), max(1, total - most), min(most, total - 1) + 1)
        return jnp.stack([one, total - one])
    sizes = jnp.asarray(length_profile(number_of, total, most, slope), jnp.int32)
    pairs = (number_of - 1) // 2
    source_of, sink = sizes[1:1 + 2 * pairs:2], sizes[2:2 + 2 * pairs:2]
    slack = jnp.minimum(source_of - 1, most - sink)
    moved = jax.random.randint(jax.random.fold_in(own_key, 1), (pairs,), 0, 1 << 20) % (slack + 1)
    sizes = sizes.at[1:1 + 2 * pairs:2].set(source_of - moved).at[2:2 + 2 * pairs:2].set(sink + moved)
    return sizes[jax.random.permutation(jax.random.fold_in(own_key, 2), number_of)]


def noise(stream_key, extent, deviation, limit, cuts=(), kind=jnp.bfloat16):
    array = jax.random.normal(stream_key, extent, jnp.float32) * deviation
    if len(cuts) > 0:
        array = levels(stream_key, extent, cuts, -0.22, 0.18) * array
    return jnp.clip(array, min=-limit, max=limit).astype(kind)


def setup_inputs(seed: int = 0) -> dict:
    streams_of = jax.random.split(jax.random.key(seed), 8)
    return {
        "hidden": noise(streams_of[0], (MICRO, TOKENS, D), 1.0, 6.0, ((1, 32),)),
        "norm_gain": jnp.clip(1.0 + 0.18 * jax.random.normal(streams_of[1], (2, D), jnp.float32), 0.1, 1.9),
        "query_weight": noise(streams_of[2], (2, D, HEADS * HEAD_DIM), D ** -0.5, 0.0625, ((0, 2), (1, 32), (2, 8))),
        "keyvalue_weight": noise(streams_of[3], (2, D, 2, KV_HEADS * HEAD_DIM), D ** -0.5, 0.0625, ((0, 2), (1, 32), (3, 8))),
        "policy_head": noise(streams_of[4], (HEADS * HEAD_DIM,), 0.05, 0.3125, ((0, 8),), jnp.float32),
        "critic_heads": noise(streams_of[5], (2, HEADS * HEAD_DIM), 0.05, 0.3125, ((1, 8),), jnp.float32),
        "lengths": jax.vmap(lambda own: uneven_parts(own, NRESP, TOKENS, LMAX, 2))(jax.random.split(streams_of[6], MICRO)).reshape((MICRO, NRESP)).astype(jnp.int32),
    }


LAMBDA_GAE = 0.95
ROPE_BASE = 1000000.0
NORM_EPS = 1e-06

def row_info(row_index, lengths_row, count_rows):
    closing = jnp.cumsum(lengths_row).astype(jnp.int32)
    opening_rows = (closing - lengths_row).astype(jnp.int32)
    response = lax.optimization_barrier(jnp.sum((row_index[:, None] >= closing[None, :]).astype(jnp.int32), axis=1))
    response = jnp.where(row_index < 0, -1, response).astype(jnp.int32)
    opening = lax.optimization_barrier(jnp.max(jnp.where(opening_rows[None, :] <= row_index[:, None], opening_rows[None, :], 0), axis=1))
    position = (row_index - opening).astype(jnp.int32)
    inside = (row_index >= 0) & (row_index < count_rows)
    finish = jnp.any(closing[None, :] == row_index[:, None] + 1, axis=1) & inside
    follows = inside & jnp.logical_not(finish)
    return (response, opening, position, finish, follows, inside)

def rotary_tables(position, head_size):
    half_size = head_size // 2
    counter = jnp.arange(half_size).astype(jnp.float32)
    inverse = jnp.exp(-jnp.log(jnp.float32(ROPE_BASE)) * (2.0 * counter / head_size))
    angles = position.astype(jnp.float32)[..., None] * inverse
    angles = jnp.concatenate([angles, angles], axis=-1)
    return (jnp.cos(angles), jnp.sin(angles))

def rotate(vectors, cosine, sine):
    half_size = vectors.shape[-1] // 2
    turned = jnp.concatenate([-vectors[..., half_size:], vectors[..., :half_size]], axis=-1)
    return vectors * cosine[..., None, :] + turned * sine[..., None, :]

def combine_maps(earlier, later):
    return (later[0] * earlier[0], later[0] * earlier[1] + later[1])

def advantage_terms(value, value_next, reward, finish, follows):
    delta = jnp.where(finish, reward, 0.0) + value_next - value
    decay = LAMBDA_GAE * follows.astype(jnp.float32)
    flipped = lax.associative_scan(combine_maps, (decay[..., ::-1], delta[..., ::-1]), axis=value.ndim - 1)
    return (flipped[0][..., ::-1], flipped[1][..., ::-1])

def section_output(hidden, gain, query_w, keyvalue_w, lengths):
    micro_count, token_count, width = hidden.shape
    kv_width = KV_HEADS * HEAD_DIM
    group_size = HEADS // KV_HEADS
    reach_rows = REACH * ROWS
    score_scale = float(HEAD_DIM) ** (-0.5)
    row_index = jnp.arange(token_count).astype(jnp.int32)
    outputs = []
    for micro_index in range(micro_count):
        rows_float = hidden[micro_index].astype(jnp.float32)
        scale = lax.rsqrt(lax.optimization_barrier(jnp.mean(rows_float * rows_float, axis=1, keepdims=True)) + NORM_EPS)
        normed = (rows_float * scale * gain[None, :]).astype(jnp.bfloat16)
        queries = jnp.dot(normed, query_w, preferred_element_type=jnp.float32)
        keyvalue = jnp.dot(normed, keyvalue_w.reshape(width, 2 * kv_width), preferred_element_type=jnp.float32)
        response, opening, position, finish, follows, inside = row_info(row_index, lengths[micro_index], token_count)
        cosine, sine = rotary_tables(position, HEAD_DIM)
        queries = rotate(queries.reshape(token_count, HEADS, HEAD_DIM), cosine, sine).astype(jnp.bfloat16)
        keys = rotate(keyvalue[:, :kv_width].reshape(token_count, KV_HEADS, HEAD_DIM), cosine, sine).astype(jnp.bfloat16)
        values = keyvalue[:, kv_width:].reshape(token_count, KV_HEADS, HEAD_DIM).astype(jnp.bfloat16)
        padded_keys = jnp.concatenate([jnp.zeros((reach_rows, KV_HEADS, HEAD_DIM), keys.dtype), keys], axis=0)
        padded_values = jnp.concatenate([jnp.zeros((reach_rows, KV_HEADS, HEAD_DIM), values.dtype), values], axis=0)
        padded_resp = jnp.concatenate([jnp.full((reach_rows,), -1, jnp.int32), response], axis=0)

        def one_block(begin):
            query_block = lax.dynamic_slice_in_dim(queries, begin, ROWS, 0).astype(jnp.float32)
            query_block = query_block.reshape(ROWS, KV_HEADS, group_size, HEAD_DIM)
            key_block = lax.dynamic_slice_in_dim(padded_keys, begin, reach_rows + ROWS, 0).astype(jnp.float32)
            value_block = lax.dynamic_slice_in_dim(padded_values, begin, reach_rows + ROWS, 0).astype(jnp.float32)
            query_resp = lax.dynamic_slice_in_dim(response, begin, ROWS, 0)
            key_resp = lax.dynamic_slice_in_dim(padded_resp, begin, reach_rows + ROWS, 0)
            query_pos = begin + jnp.arange(ROWS).astype(jnp.int32)
            key_pos = begin - reach_rows + jnp.arange(reach_rows + ROWS).astype(jnp.int32)
            scores = jnp.einsum('rkgd,skd->kgrs', query_block, key_block) * score_scale
            allowed = (query_resp[:, None] == key_resp[None, :]) & (key_pos[None, :] <= query_pos[:, None])
            weights = jnp.where(allowed[None, None], jnp.exp(scores), 0.0)
            probs = (weights / lax.optimization_barrier(jnp.sum(weights, axis=-1, keepdims=True))).astype(jnp.bfloat16)
            attended = jnp.einsum('kgrs,skd->rkgd', probs.astype(jnp.float32), value_block)
            return attended.reshape(ROWS, HEADS * HEAD_DIM)
        block_starts = (jnp.arange(token_count // ROWS) * ROWS).astype(jnp.int32)
        outputs.append(lax.map(one_block, block_starts).reshape(token_count, HEADS * HEAD_DIM))
    return jnp.stack(outputs, axis=0)

def reference(hidden, norm_gain, query_weight, keyvalue_weight, policy_head, critic_heads, lengths):
    actor = section_output(hidden, norm_gain[0], query_weight[0], keyvalue_weight[0], lengths)
    critic = section_output(hidden, norm_gain[1], query_weight[1], keyvalue_weight[1], lengths)
    policy_scores = jnp.dot(actor, policy_head, precision=lax.Precision.HIGHEST)
    value = jnp.dot(critic, critic_heads[0], precision=lax.Precision.HIGHEST)
    reward = jnp.dot(critic, critic_heads[1], precision=lax.Precision.HIGHEST)
    micro_count, token_count = value.shape
    row_index = jnp.arange(token_count).astype(jnp.int32)
    advantage_rows = []
    for micro_index in range(micro_count):
        response, opening, position, finish, follows, inside = row_info(row_index, lengths[micro_index], token_count)
        value_row = value[micro_index]
        value_next = jnp.concatenate([value_row[1:], jnp.zeros((1,), jnp.float32)]) * follows.astype(jnp.float32)
        decay_sum, advantage = advantage_terms(value_row, value_next, reward[micro_index], finish, follows)
        advantage_rows.append(advantage)
    advantages = jnp.stack(advantage_rows, axis=0)
    returns = advantages + value
    return (policy_scores, advantages, returns)
```

```python
import functools

import jax
import jax.numpy as jnp
from jax import lax
from jax.experimental import pallas as pl
from jax.experimental.pallas import tpu as pltpu
from jax.sharding import PartitionSpec as P

F32 = jnp.float32
BF16 = jnp.bfloat16
MESH = pl.DeviceIdType.MESH
HIGHEST = lax.Precision.HIGHEST

HD = 128
NX, NY, NZ = 4, 8, 8
ROWS = 144
BLOCK = 288
GROUP = 576
WINDOW = 864
WIDTH = 8192
PIECE = 256
NRESP = 64
LAMBDA_GAE = 0.95
LOG_LAMBDA = -0.05129329438755058
LOG_BASE = 13.815510557964274
NORM_EPS = 1e-06
SCALE = float(HD) ** -0.5

REL = (0, 1, -1, 2, -2, 3, -3, 4)
PLACE = {0: 0, 1: 1, -1: 2, 2: 3, -2: 4, 3: 5, -3: 6, 4: 7, -4: 7}


def rel_of(place):
    return ((place + 1) // 2) * (2 * (place % 2) - 1)


def remote(src, dst, send, recv, device):
    copy = pltpu.make_async_remote_copy(
        src_ref=src, dst_ref=dst, send_sem=send, recv_sem=recv, device_id=device, device_id_type=MESH
    )
    copy.start()


def local(src, dst, sem):
    pltpu.make_async_copy(src, dst, sem).start()


def take(ref, sem):
    pltpu.make_async_copy(ref, ref, sem).wait()


def iota(shape, axis):
    return lax.broadcasted_iota(jnp.int32, shape, axis)


def dot(a, b, over, precision=None):
    return lax.dot_general(
        a, b, ((over[0], over[1]), ((), ())), precision=precision, preferred_element_type=F32
    )


def closing_row(lengths):
    upto = (iota((NRESP, NRESP), 0) <= iota((NRESP, NRESP), 1)).astype(F32)
    return dot(lengths, upto, ((1,), (0,)), HIGHEST)


def closing_column(lengths):
    upto = (iota((NRESP, NRESP), 1) <= iota((NRESP, NRESP), 0)).astype(F32)
    return dot(upto, lengths, ((1,), (1,)), HIGHEST)


def places():
    s = lax.axis_index("sec")
    q = lax.axis_index("seq")
    z = lax.axis_index("mp")
    return s, q % NX, q // NX, z


def at(s, x, y, z):
    return (s, y * NX + x, z)


def section_kernel(
    hid, gain, qw, kvw, policy, critic, lengths, out,
    hbuf, raw, normed, wts, scales, own, side, rs_out, rs_in, rl_out, rl_in,
    queries, window, attended,
    sem_loc, send_a, recv_a, send_d, recv_d, send_z, recv_z, send_c, recv_c,
    send_s, recv_s, send_b, recv_b, send_l, recv_l, send_r, recv_r, send_h, recv_h,
):
    s, x, y, z = places()
    micro, half = x // 2, x % 2
    other = 1 - s

    def chip(dx=0, dy=0):
        return at(s, (x + dx + NX) % NX, (y + dy + NY) % NY, z)

    diagonal = at(s, 2 * micro + 1 - half, (y + 2 * half - 1 + NY) % NY, z)
    ring_z = [at(s, x, y, (z + 1) % NZ), at(s, x, y, (z + NZ - 1) % NZ)]
    ring_y = [chip(dy=1), chip(dy=-1)]
    sibling = at(other, x, y, z)

    barrier = pltpu.get_barrier_semaphore()
    partners = [at((s + ds) % 2, (x + dx) % NX, y, z) for ds in range(2) for dx in range(NX)][1:]
    partners = partners + ring_y + ring_z + [diagonal]
    for device in partners:
        pl.semaphore_signal(barrier, inc=1, device_id=device, device_id_type=MESH)
    pl.semaphore_wait(barrier, len(partners))

    def column(place, xx):
        start = ((y + rel_of(place) + NY) % NY) * (NX * PIECE) + xx * PIECE
        return pl.ds(pl.multiple_of(start, PIECE), PIECE)

    facing = (x + 2) % NX
    remote(hid.at[s, :, column(z, facing)], raw.at[0, 2, z], send_d, recv_d, chip(dx=2))
    local(hid.at[s], hbuf, sem_loc.at[0])

    def weights(c, place, piece=None):
        begin, size = place * PIECE, PIECE
        if piece is not None:
            begin, size = begin + piece * (PIECE // 2), PIECE // 2
        return wts.at[c, pl.ds(begin, size)]

    mine = (kvw, qw.at[:, pl.ds(0, PIECE)], qw.at[:, pl.ds(PIECE, PIECE)])

    def ring_send(c, step):
        for d, sign in ((0, 1), (1, -1)):
            piece = d if step == 4 else None
            target = weights(c, PLACE[-sign * step], piece)
            source = mine[c] if step == 1 else weights(c, PLACE[-sign * (step - 1)], piece)
            remote(source, target, send_b.at[c, step - 1, d], recv_b.at[c, step - 1, d], ring_y[d])

    def ring_take(c, step, sems=None):
        sems = recv_b if sems is None else sems
        for d, sign in ((0, 1), (1, -1)):
            piece = d if step == 4 else None
            take(weights(c, PLACE[-sign * step], piece), sems.at[c, step - 1, d])

    ring_send(0, 1)

    for place in range(NY):
        for d, dx in ((0, 1), (1, NX - 1)):
            remote(
                hid.at[s, :, column(place, (x + dx) % NX)],
                raw.at[0, NX - dx, place],
                send_a.at[d],
                recv_a.at[d],
                chip(dx=dx),
            )
        if place == 1:
            ring_send(1, 1)
    for place in range(NY):
        local(hid.at[s, :, column(place, x)], raw.at[0, 0, place], sem_loc.at[1])
        local(hid.at[other, :, column(place, x)], raw.at[1, 0, place], sem_loc.at[2])
    for c in range(3):
        local(mine[c], weights(c, 0), sem_loc.at[3 + c])

    take(hbuf, sem_loc.at[0])

    def squares(i, total):
        for j in range(4):
            start = pl.multiple_of((i * 4 + j) * HD, HD)
            part = hbuf[:, pl.ds(start, HD)].astype(F32)
            total = total + part * part
        return total

    total = lax.fori_loop(0, WIDTH // HD // 4, squares, jnp.zeros((ROWS, HD), F32))
    mean = dot(jnp.ones((8, HD), F32), total, ((1,), (1,)), HIGHEST) * (1.0 / WIDTH)
    scales[0] = lax.rsqrt(mean + NORM_EPS)
    for ds in range(2):
        for dx in range(NX):
            if ds + dx > 0:
                slot = ((2 - ds) % 2) * NX + (NX - dx) % NX
                remote(
                    scales.at[0], scales.at[slot], send_s, recv_s, at((s + ds) % 2, (x + dx) % NX, y, z)
                )

    def z_shard(index, d, step):
        shard = raw.at[0, 2, (index + 2 * NZ) % NZ]
        if step == 4:
            shard = shard.at[:, pl.ds(d * HD, HD)]
        return shard

    def z_send(step):
        for d, sign in ((0, 1), (1, -1)):
            shard = z_shard(z - sign * (step - 1), d, step)
            remote(shard, shard, send_z.at[step - 1, d], recv_z.at[step - 1, d], ring_z[d])

    def z_take(step, sems=None):
        sems = recv_z if sems is None else sems
        for d, sign in ((0, 1), (1, -1)):
            take(z_shard(z - sign * step, d, step), sems.at[step - 1, d])

    take(raw.at[0, 2, z], recv_d)
    z_send(1)
    ring_take(0, 1)
    ring_send(0, 2)
    ring_send(2, 1)

    lens = lengths[...].astype(F32)
    closings = closing_row(lens)
    openings = closings - lens
    opening_line = jnp.where(micro == 0, openings[0:1], openings[1:2])
    row = (y * GROUP + half * BLOCK + iota((BLOCK, 1), 0)).astype(F32)
    opening = jnp.max(jnp.where(opening_line <= row, opening_line, 0.0), axis=1, keepdims=True)
    lane = iota((1, HD), 1)
    inverse = jnp.exp((lane % (HD // 2)).astype(F32) * (-2.0 * LOG_BASE / HD))
    angle = (row - opening) * inverse
    cosine = jnp.cos(angle)
    sine = jnp.sin(angle) * jnp.where(lane < HD // 2, -1.0, 1.0)

    def rotated(v):
        return (v * cosine + pltpu.roll(v, HD // 2, 1) * sine).astype(BF16)

    take(scales.at[pl.ds(1, 7)], recv_s)

    def normalise(ds, dx):
        base = (((s + ds) % 2) * NX + (x + dx) % NX) * ROWS
        rows = pl.ds(pl.multiple_of(base, 16), ROWS)
        spread = (iota((8, PIECE), 0) == 0).astype(F32)
        scale = dot(scales[ds * NX + dx], spread, ((0,), (0,)), HIGHEST)

        def one(place, carry):
            part = raw[ds, dx, place].astype(F32) * scale * gain[0:1, column(place, x)]
            normed[rows, pl.ds(pl.multiple_of(place * PIECE, PIECE), PIECE)] = part.astype(BF16)
            return carry

        lax.fori_loop(0, NY, one, 0)

    def to_sibling(dx):
        remote(raw.at[0, dx], raw.at[1, dx], send_c.at[dx - 1], recv_c.at[dx - 1], sibling)

    z_take(1)
    z_send(2)
    take(raw.at[0, 0], sem_loc.at[1])
    normalise(0, 0)
    ring_take(0, 2)
    ring_send(0, 3)
    z_take(2)
    z_send(3)
    take(raw.at[1, 0], sem_loc.at[2])
    normalise(1, 0)
    ring_take(1, 1)
    ring_send(1, 2)
    z_take(3)
    z_send(4)
    ring_take(0, 3)
    ring_send(0, 4)
    z_take(4)
    to_sibling(2)
    normalise(0, 2)
    ring_take(2, 1)
    ring_send(2, 2)
    take(raw.at[0, 3], recv_a.at[0])
    to_sibling(3)
    take(raw.at[0, 1], recv_a.at[1])
    to_sibling(1)
    ring_take(1, 2)
    ring_send(1, 3)
    normalise(0, 3)
    normalise(0, 1)
    for dx in (2, 3, 1):
        take(raw.at[1, dx], recv_c.at[dx - 1])
        normalise(1, dx)

    def partial(c, xx):
        rows = pl.ds(pl.multiple_of(xx * BLOCK, 32), BLOCK)
        return dot(normed[rows, :], wts[c], ((1,), (0,)))

    def project(c):
        far = partial(c, facing).astype(BF16)
        for d, dx in ((0, 1), (1, NX - 1)):
            rl_out[c, d] = far[:, d * HD : (d + 1) * HD]
            remote(rl_out.at[c, d], rl_in.at[c, d], send_l.at[c, d], recv_l.at[c, d], chip(dx=dx))
        side[c, 0] = partial(c, (x + 1) % NX)
        side[c, 1] = partial(c, (x + NX - 1) % NX)
        own[c] = partial(c, x)

    def pass_on(c):
        for d, dx in ((0, 1), (1, NX - 1)):
            take(rl_in.at[c, d], recv_l.at[c, d])
            both = slice(d * HD, (d + 1) * HD)
            rest = slice((1 - d) * HD, (2 - d) * HD)
            rs_out[c, d, :, both] = (side[c, d, :, both] + rl_in[c, d].astype(F32)).astype(BF16)
            rs_out[c, d, :, rest] = side[c, d, :, rest].astype(BF16)
            remote(rs_out.at[c, d], rs_in.at[c, d], send_r.at[c, d], recv_r.at[c, d], chip(dx=dx))

    def collect(c):
        for d in range(2):
            take(rs_in.at[c, d], recv_r.at[c, d])
        return own[c] + rs_in[c, 0].astype(F32) + rs_in[c, 1].astype(F32)

    for c in range(3):
        take(weights(c, 0), sem_loc.at[3 + c])

    ring_take(0, 4)
    project(0)
    ring_take(2, 2)
    ring_send(2, 3)
    ring_take(1, 3)
    ring_send(1, 4)
    pass_on(0)
    ring_take(1, 4)
    project(1)
    ring_take(2, 3)
    ring_send(2, 4)

    keyvalue = collect(0)
    window[pl.ds(2 * BLOCK, BLOCK), 0:HD] = rotated(keyvalue[:, 0:HD])
    window[pl.ds(2 * BLOCK, BLOCK), HD : 2 * HD] = keyvalue[:, HD : 2 * HD].astype(BF16)
    next_block = at(s, 2 * micro + 1 - half, (y + half) % NY, z)
    for i, device in ((0, chip(dy=1)), (1, next_block)):
        remote(
            window.at[pl.ds(2 * BLOCK, BLOCK)],
            window.at[pl.ds(i * BLOCK, BLOCK)],
            send_h.at[i],
            recv_h.at[i],
            device,
        )
    pass_on(1)
    ring_take(2, 4)
    project(2)

    def store_queries(c):
        pair = collect(c)
        queries[2 * (c - 1)] = rotated(pair[:, 0:HD])
        queries[2 * (c - 1) + 1] = rotated(pair[:, HD : 2 * HD])

    store_queries(1)
    for i in range(2):
        take(window.at[pl.ds(i * BLOCK, BLOCK)], recv_h.at[i])

    key_row = (y * GROUP + half * BLOCK - GROUP + iota((1, WINDOW), 1)).astype(F32)

    def attend(head):
        scores = dot(queries[head], window[:, 0:HD], ((1,), (1,))) * SCALE
        allowed = (key_row >= opening) & (key_row <= row)
        weight = jnp.where(allowed, jnp.exp(scores), 0.0)
        probs = (weight / jnp.sum(weight, axis=1, keepdims=True)).astype(BF16)
        attended[:, head * HD : (head + 1) * HD] = dot(probs, window[:, HD : 2 * HD], ((1,), (0,)))

    attend(0)
    pass_on(2)
    attend(1)
    store_queries(2)
    attend(2)
    attend(3)

    actor = jnp.where(s == 0, 1.0, 0.0)
    kind = iota((8, 4 * HD), 0)
    heads = jnp.where(kind == 0, policy[...] * actor, 0.0)
    heads = jnp.where(kind == 1, critic[0:1] * (1.0 - actor), heads)
    heads = jnp.where(kind == 2, critic[1:2] * (1.0 - actor), heads)
    out[...] = dot(heads, attended[...], ((1,), (1,)), HIGHEST)

    take(raw.at[0, 2, z], send_d)
    for d, dx in ((0, 1), (1, NX - 1)):
        take(raw.at[0, NX - dx], send_a.at[d])
    take(scales.at[pl.ds(1, 7)], send_s)
    for step in range(1, 5):
        z_take(step, send_z)
        for c in range(3):
            ring_take(c, step, send_b)
    for dx in (1, 2, 3):
        take(raw.at[1, dx], send_c.at[dx - 1])
    for c in range(3):
        for d in range(2):
            take(rl_out.at[c, d], send_l.at[c, d])
            take(rs_out.at[c, d], send_r.at[c, d])
    for i in range(2):
        take(window.at[pl.ds(i * BLOCK, BLOCK)], send_h.at[i])


def score_kernel(part, lengths, scores_out, adv_out, ret_out, terms, blocks, send_t, recv_t, send_g, recv_g):
    s, x, y, z = places()

    def chip(dx=0, dy=0):
        return at(s, (x + dx) % NX, (y + dy + NY) % NY, z)

    others = [(ds, dz) for ds in range(2) for dz in range(NZ)][1:]
    stack = [at((s + ds) % 2, x, y, (z + dz) % NZ) for ds, dz in others]
    barrier = pltpu.get_barrier_semaphore()
    partners = stack + [chip(dx, 0) for dx in range(1, NX)]
    partners = partners + [chip(dx, dy) for dx in range(NX) for dy in (-1, 1)]
    for device in partners:
        pl.semaphore_signal(barrier, inc=1, device_id=device, device_id_type=MESH)
    pl.semaphore_wait(barrier, len(partners))

    for (ds, dz), device in zip(others, stack):
        slot = ((2 - ds) % 2) * NZ + (NZ - dz) % NZ - 1
        remote(part, terms.at[slot], send_t, recv_t, device)

    lens = lengths[...].astype(F32)
    closings = closing_column(lens) - (y * GROUP).astype(F32)

    take(terms, recv_t)
    total = part[...]
    for i in range(15):
        total = total + terms[i]
    blocks[0, x] = total
    sends = [(dx, 0) for dx in range(1, NX)] + [(dx, 1) for dx in range(NX)]
    for dx, back in sends:
        remote(blocks.at[0, x], blocks.at[back, x], send_g.at[back, dx], recv_g.at[back, dx], chip(dx, -back))

    now = (x * ROWS + iota((1, ROWS), 1)).astype(F32)
    ends = []
    for m in range(2):
        line = closings[:, m : m + 1]
        ends.append(jnp.min(jnp.where(line > now, line, 1e9), axis=0, keepdims=True))

    for dx, back in sends:
        take(blocks.at[back, (x + NX - dx) % NX], recv_g.at[back, dx])

    for m in range(2):
        kept = jnp.zeros((8, ROWS), F32)
        summed = jnp.zeros((8, ROWS), F32)
        rewarded = jnp.zeros((8, ROWS), F32)
        for back in range(2):
            for h in range(2):
                block = blocks[back, 2 * m + h]
                then = ((2 * back + h) * BLOCK + iota((BLOCK, 1), 0)).astype(F32)
                ahead = then - now
                inside = (ahead >= 0.0) & (then < ends[m])
                power = jnp.exp(jnp.maximum(ahead, 0.0) * LOG_LAMBDA)
                same = (ahead == 0.0).astype(F32)
                later = power * ((1.0 - LAMBDA_GAE) / LAMBDA_GAE)
                value_part = jnp.where(inside, jnp.where(ahead == 0.0, -1.0, later), 0.0)
                reward_part = jnp.where(inside & (then + 1.0 == ends[m]), power, 0.0)
                if back == 0:
                    kept = kept + dot(block, same, ((1,), (0,)), HIGHEST)
                summed = summed + dot(block, value_part, ((1,), (0,)), HIGHEST)
                rewarded = rewarded + dot(block, reward_part, ((1,), (0,)), HIGHEST)
        advantage = summed[1:2] + rewarded[2:3]
        scores_out[m : m + 1, :] = kept[0:1]
        adv_out[m : m + 1, :] = advantage
        ret_out[m : m + 1, :] = advantage + kept[1:2]

    take(terms, send_t)
    for dx, back in sends:
        take(blocks.at[0, x], send_g.at[back, dx])


def on_device(hidden, norm_gain, query_weight, keyvalue_weight, policy_head, critic_heads, lengths):
    vmem = pl.BlockSpec(memory_space=pltpu.VMEM)
    hbm = pl.BlockSpec(memory_space=pl.ANY)
    dma = pltpu.SemaphoreType.DMA
    part = pl.pallas_call(
        section_kernel,
        out_shape=jax.ShapeDtypeStruct((8, BLOCK), F32),
        in_specs=[hbm, vmem, hbm, hbm, vmem, vmem, vmem],
        out_specs=vmem,
        scratch_shapes=[
            pltpu.VMEM((ROWS, WIDTH), BF16),
            pltpu.VMEM((2, NX, NY, ROWS, PIECE), BF16),
            pltpu.VMEM((2 * GROUP, NY * PIECE), BF16),
            pltpu.VMEM((3, NY * PIECE, PIECE), BF16),
            pltpu.VMEM((8, 8, ROWS), F32),
            pltpu.VMEM((3, BLOCK, PIECE), F32),
            pltpu.VMEM((3, 2, BLOCK, PIECE), F32),
            pltpu.VMEM((3, 2, BLOCK, PIECE), BF16),
            pltpu.VMEM((3, 2, BLOCK, PIECE), BF16),
            pltpu.VMEM((3, 2, BLOCK, HD), BF16),
            pltpu.VMEM((3, 2, BLOCK, HD), BF16),
            pltpu.VMEM((4, BLOCK, HD), BF16),
            pltpu.VMEM((WINDOW, PIECE), BF16),
            pltpu.VMEM((BLOCK, 4 * HD), F32),
            dma((6,)), dma((2,)), dma((2,)), dma, dma, dma((4, 2)), dma((4, 2)), dma((3,)), dma((3,)),
            dma, dma, dma((3, 4, 2)), dma((3, 4, 2)), dma((3, 2)), dma((3, 2)), dma((3, 2)), dma((3, 2)),
            dma((2,)), dma((2,)),
        ],
        compiler_params=pltpu.CompilerParams(
            collective_id=0, has_side_effects=True, vmem_limit_bytes=48 * 1024 * 1024
        ),
        name="section",
    )(
        hidden,
        norm_gain,
        query_weight[0],
        keyvalue_weight[0].reshape(PIECE, 2 * HD),
        policy_head.reshape(1, -1),
        critic_heads,
        lengths,
    )
    line = jax.ShapeDtypeStruct((2, ROWS), F32)
    return pl.pallas_call(
        score_kernel,
        out_shape=(line, line, line),
        in_specs=[vmem, vmem],
        out_specs=(vmem, vmem, vmem),
        scratch_shapes=[
            pltpu.VMEM((15, 8, BLOCK), F32),
            pltpu.VMEM((2, NX, 8, BLOCK), F32),
            dma, dma, dma((2, NX)), dma((2, NX)),
        ],
        compiler_params=pltpu.CompilerParams(collective_id=1, has_side_effects=True),
        name="scores",
    )(part, lengths)


def solution(mesh):
    placed = (
        P(None, "seq", None),
        P("sec", None),
        P("sec", "seq", "mp"),
        P("sec", "seq", None, "mp"),
        P("mp"),
        P(None, "mp"),
        P(),
    )
    return jax.shard_map(
        on_device,
        mesh=mesh,
        in_specs=placed,
        out_specs=(P(None, "seq"), P(None, "seq"), P(None, "seq")),
        check_vma=False,
    )
```

```python
import functools

import jax
import jax.numpy as jnp
from jax import lax
from jax.experimental import pallas as pl
from jax.experimental.pallas import tpu as pltpu
from jax.sharding import PartitionSpec as P

F32 = jnp.float32
BF16 = jnp.bfloat16
MESH = pl.DeviceIdType.MESH
HIGHEST = lax.Precision.HIGHEST

HD = 128
NX, NY, NZ = 4, 8, 8
ROWS = 144
BLOCK = 288
GROUP = 576
WINDOW = 864
WIDTH = 8192
PIECE = 256
NRESP = 64
LANES = 384
PIECES = 6
LAMBDA_GAE = 0.95
LOG_LAMBDA = -0.05129329438755058
LOG_BASE = 13.815510557964274
NORM_EPS = 1e-06
SCALE = float(HD) ** -0.5

REL = (0, 1, -1, 2, -2, 3, -3, 4)
PLACE = {0: 0, 1: 1, -1: 2, 2: 3, -2: 4, 3: 5, -3: 6, 4: 7, -4: 7}


def rel_of(place):
    return ((place + 1) // 2) * (2 * (place % 2) - 1)


def remote(src, dst, send, recv, device):
    copy = pltpu.make_async_remote_copy(
        src_ref=src, dst_ref=dst, send_sem=send, recv_sem=recv, device_id=device, device_id_type=MESH
    )
    copy.start()


def local(src, dst, sem):
    pltpu.make_async_copy(src, dst, sem).start()


def take(ref, sem):
    pltpu.make_async_copy(ref, ref, sem).wait()


def iota(shape, axis):
    return lax.broadcasted_iota(jnp.int32, shape, axis)


def dot(a, b, over, precision=None):
    return lax.dot_general(
        a, b, ((over[0], over[1]), ((), ())), precision=precision, preferred_element_type=F32
    )


def chain(refs):
    return jnp.concatenate([refs[i : i + 1] for i in range(3)], axis=1)


def closing_row(lengths):
    upto = (iota((NRESP, NRESP), 0) <= iota((NRESP, NRESP), 1)).astype(F32)
    return dot(lengths, upto, ((1,), (0,)), HIGHEST)


def closing_column(lengths):
    upto = (iota((NRESP, NRESP), 1) <= iota((NRESP, NRESP), 0)).astype(F32)
    return dot(upto, lengths, ((1,), (1,)), HIGHEST)


def places():
    s = lax.axis_index("sec")
    q = lax.axis_index("seq")
    z = lax.axis_index("mp")
    return s, q % NX, q // NX, z


def at(s, x, y, z):
    return (s, y * NX + x, z)


def section_kernel(
    hid, gain_hbm, qw, kvw, policy_hbm, critic_hbm, lengths_hbm, out,
    hbuf, raw, normed, wts, scales, gain, policy, critic, lengths,
    own_kv, own_q, out_kv, in_kv, out_q, in_q, queries, window, attended, part, tile, terms, results, blocks, scores,
    sem_loc, send_a, recv_a, send_d, recv_d, send_z, recv_z, send_c, recv_c, send_s, recv_s, send_b, recv_b,
    send_kv, recv_kv, send_q, recv_q, send_h, recv_h, send_t, recv_t, send_g, recv_g, recv_p,
):
    s, x, y, z = places()
    micro, half = x // 2, x % 2
    other = 1 - s

    def chip(dx=0, dy=0, core=None):
        return at(s if core is None else core, (x + dx) % NX, (y + dy + NY) % NY, z)

    def over_z(dz):
        return at(s, x, y, (z + dz + NZ) % NZ)

    sibling = at(other, x, y, z)
    barrier = pltpu.get_barrier_semaphore()
    partners = [chip(dx, 0, (s + ds) % 2) for ds in range(2) for dx in range(NX)][1:]
    partners = partners + [chip(dx, dy, core) for core in range(2) for dx in range(NX) for dy in (-1, 1)]
    partners = partners + [over_z(dz) for dz in range(1, NZ)]
    for device in partners:
        pl.semaphore_signal(barrier, inc=1, device_id=device, device_id_type=MESH)
    pl.semaphore_wait(barrier, len(partners))

    def column(place, xx):
        start = ((y + rel_of(place) + NY) % NY) * (NX * PIECE) + xx * PIECE
        return pl.ds(pl.multiple_of(start, PIECE), PIECE)

    facing = (x + 2) % NX
    quarter = z % 4
    for i in range(2):
        remote(
            hid.at[s, :, column(2 * quarter + i, facing)], raw.at[0, 2, 2 * quarter + i], send_d, recv_d, chip(2)
        )

    def weights(p, place, piece=None):
        begin, size = place * PIECE, PIECE
        if piece is not None:
            begin, size = begin + piece * (PIECE // 2), PIECE // 2
        return wts.at[p // 2, pl.ds(begin, size), pl.ds((p % 2) * HD, HD)]

    def mine(p):
        return kvw.at[:, pl.ds(p * HD, HD)] if p < 2 else qw.at[:, pl.ds((p - 2) * HD, HD)]

    ring_y = [chip(0, 1), chip(0, -1)]

    def ring_send(p, step):
        for d, sign in ((0, 1), (1, -1)):
            piece = d if step == 4 else None
            target = weights(p, PLACE[-sign * step], piece)
            source = mine(p) if step == 1 else weights(p, PLACE[-sign * (step - 1)], piece)
            remote(source, target, send_b.at[p, step - 1, d], recv_b.at[p, step - 1, d], ring_y[d])

    def ring_take(p, step, sems=None):
        sems = recv_b if sems is None else sems
        for d, sign in ((0, 1), (1, -1)):
            piece = d if step == 4 else None
            take(weights(p, PLACE[-sign * step], piece), sems.at[p, step - 1, d])

    def ring(p, step):
        ring_take(p, step)
        ring_send(p, step + 1)

    def to_neighbours(place):
        for d, dx in ((0, 1), (1, NX - 1)):
            remote(
                hid.at[s, :, column(place, (x + dx) % NX)],
                raw.at[0, NX - dx, place],
                send_a.at[d],
                recv_a.at[d],
                chip(dx),
            )

    ring_send(0, 1)
    ring_send(1, 1)
    for place in range(4):
        to_neighbours(place)
    ring_send(2, 1)
    for place in range(4, NY):
        to_neighbours(place)
    local(hid.at[s], hbuf, sem_loc.at[0])
    local(gain_hbm, gain, sem_loc.at[1])
    local(policy_hbm, policy, sem_loc.at[2])
    local(critic_hbm, critic, sem_loc.at[3])
    local(lengths_hbm, lengths, sem_loc.at[4])
    for place in range(NY):
        local(hid.at[s, :, column(place, x)], raw.at[0, 0, place], sem_loc.at[5])
        local(hid.at[other, :, column(place, x)], raw.at[1, 0, place], sem_loc.at[6])
    local(kvw, wts.at[0, pl.ds(0, PIECE)], sem_loc.at[7])
    for i in range(2):
        local(qw.at[:, pl.ds(i * PIECE, PIECE)], wts.at[i + 1, pl.ds(0, PIECE)], sem_loc.at[8 + i])

    def quarters(t, i=None):
        begin = 2 * ((t + 4) % 4)
        return raw.at[0, 2, pl.ds(begin, 2)] if i is None else raw.at[0, 2, begin + i]

    spread = ((1, None), (-1, None), (2, 1), (-2, 0))
    take(quarters(quarter), recv_d)
    for n, (dz, i) in enumerate(spread):
        remote(quarters(quarter, i), quarters(quarter, i), send_z.at[n], recv_z.at[n], over_z(dz))

    take(hbuf, sem_loc.at[0])

    def squares(i, total):
        for j in range(4):
            start = pl.multiple_of((i * 4 + j) * HD, HD)
            block = hbuf[:, pl.ds(start, HD)].astype(F32)
            total = total + block * block
        return total

    total = lax.fori_loop(0, WIDTH // HD // 4, squares, jnp.zeros((ROWS, HD), F32))
    mean = dot(jnp.ones((8, HD), F32), total, ((1,), (1,)), HIGHEST) * (1.0 / WIDTH)
    scales[0] = lax.rsqrt(mean + NORM_EPS)
    for ds in range(2):
        for dx in range(NX):
            if ds + dx > 0:
                slot = ((2 - ds) % 2) * NX + (NX - dx) % NX
                remote(scales.at[0], scales.at[slot], send_s, recv_s, chip(dx, 0, (s + ds) % 2))

    ring(0, 1)
    ring(1, 1)
    ring(2, 1)

    take(lengths, sem_loc.at[4])
    lens = lengths[...].astype(F32)
    openings = closing_row(lens) - lens
    opening_line = jnp.where(micro == 0, openings[0:1], openings[1:2])
    row = (y * GROUP + half * BLOCK + iota((BLOCK, 1), 0)).astype(F32)
    opening = jnp.max(jnp.where(opening_line <= row, opening_line, 0.0), axis=1, keepdims=True)
    lane = iota((1, HD), 1)
    inverse = jnp.exp((lane % (HD // 2)).astype(F32) * (-2.0 * LOG_BASE / HD))
    angle = (row - opening) * inverse
    cosine = jnp.cos(angle)
    sine = jnp.sin(angle) * jnp.where(lane < HD // 2, -1.0, 1.0)

    def rotated(v):
        return (v * cosine + pltpu.roll(v, HD // 2, 1) * sine).astype(BF16)

    take(policy, sem_loc.at[2])
    take(critic, sem_loc.at[3])
    kind = iota((8, 4 * HD), 0)
    first = jnp.where(s == 0, policy[...], critic[0:1])
    second = jnp.where(s == 0, 0.0, critic[1:2])
    heads = jnp.where(kind == 0, first, jnp.where(kind == 1, second, 0.0))
    attended[pl.ds(BLOCK, LANES - BLOCK), :] = jnp.zeros((LANES - BLOCK, HD), F32)

    take(scales.at[pl.ds(1, 7)], recv_s)
    take(gain, sem_loc.at[1])

    def normalise(ds, dx):
        base = (((s + ds) % 2) * NX + (x + dx) % NX) * ROWS
        rows = pl.ds(pl.multiple_of(base, 16), ROWS)
        first_row = (iota((8, PIECE), 0) == 0).astype(F32)
        scale = dot(scales[ds * NX + dx], first_row, ((0,), (0,)), HIGHEST)

        def one(place, carry):
            block = raw[ds, dx, place].astype(F32) * scale * gain[0:1, column(place, x)]
            normed[rows, pl.ds(pl.multiple_of(place * PIECE, PIECE), PIECE)] = block.astype(BF16)
            return carry

        lax.fori_loop(0, NY, one, 0)

    def to_sibling(dx):
        remote(raw.at[0, dx], raw.at[1, dx], send_c.at[dx - 1], recv_c.at[dx - 1], sibling)

    def from_sibling(dx):
        take(raw.at[1, dx], recv_c.at[dx - 1])
        normalise(1, dx)

    take(raw.at[0, 0], sem_loc.at[5])
    normalise(0, 0)
    ring(0, 2)
    take(raw.at[1, 0], sem_loc.at[6])
    normalise(1, 0)
    ring(1, 2)
    ring(2, 2)
    ring(0, 3)
    ring_send(3, 1)
    take(raw.at[0, 3], recv_a.at[0])
    to_sibling(3)
    normalise(0, 3)
    ring(1, 3)
    ring_send(4, 1)
    take(raw.at[0, 1], recv_a.at[1])
    to_sibling(1)
    normalise(0, 1)
    ring(2, 3)
    ring_send(5, 1)
    for n, (dz, i) in enumerate(spread):
        take(quarters(quarter - dz, i), recv_z.at[n])
    to_sibling(2)
    normalise(0, 2)
    from_sibling(3)
    ring(3, 1)
    from_sibling(1)
    ring(4, 1)
    from_sibling(2)
    ring(5, 1)

    def rows_of(dx):
        return pl.ds(pl.multiple_of(((x + dx) % NX) * BLOCK, 32), BLOCK)

    def project_kv(dx):
        product = dot(normed[rows_of(dx), :], wts[0], ((1,), (0,)))
        if dx == 0:
            own_kv[...] = product
        else:
            out_kv[dx - 1] = product.astype(BF16)
            remote(out_kv.at[dx - 1], in_kv.at[dx - 1], send_kv.at[dx - 1], recv_kv.at[dx - 1], chip(dx))

    def project_q(head, dx):
        piece = wts[1 + head // 2, :, (head % 2) * HD : (head % 2 + 1) * HD]
        product = dot(normed[rows_of(dx), :], piece, ((1,), (0,)))
        if dx == 0:
            own_q[head] = product
        else:
            out_q[head, dx - 1] = product.astype(BF16)
            remote(
                out_q.at[head, dx - 1],
                in_q.at[head, dx - 1],
                send_q.at[head, dx - 1],
                recv_q.at[head, dx - 1],
                chip(dx),
            )

    def query(head):
        for dx in range(3):
            take(in_q.at[head, dx], recv_q.at[head, dx])
        summed = own_q[head]
        for dx in range(3):
            summed = summed + in_q[head, dx].astype(F32)
        queries[head] = rotated(summed)

    for i in range(3):
        take(wts.at[i, pl.ds(0, PIECE)], sem_loc.at[7 + i])
    ring_take(0, 4)
    ring_take(1, 4)
    project_kv(2)
    ring(3, 2)
    project_kv(1)
    project_kv(3)
    ring(4, 2)
    project_kv(0)
    ring(5, 2)
    ring_take(2, 4)
    project_q(0, 2)
    project_q(0, 1)
    ring(3, 3)
    project_q(0, 3)
    project_q(0, 0)
    ring(4, 3)

    for dx in range(3):
        take(in_kv.at[dx], recv_kv.at[dx])
    keyvalue = own_kv[...]
    for dx in range(3):
        keyvalue = keyvalue + in_kv[dx].astype(F32)
    window[pl.ds(2 * BLOCK, BLOCK), 0:HD] = rotated(keyvalue[:, 0:HD])
    window[pl.ds(2 * BLOCK, BLOCK), HD : 2 * HD] = keyvalue[:, HD : 2 * HD].astype(BF16)
    next_block = at(s, 2 * micro + 1 - half, (y + half) % NY, z)
    for i, device in ((0, chip(0, 1)), (1, next_block)):
        remote(
            window.at[pl.ds(2 * BLOCK, BLOCK)],
            window.at[pl.ds(i * BLOCK, BLOCK)],
            send_h.at[i],
            recv_h.at[i],
            device,
        )
    ring(5, 3)
    ring_take(3, 4)
    for dx in (2, 1, 3, 0):
        project_q(1, dx)
    query(0)
    ring_take(4, 4)
    for dx in (2, 1, 3, 0):
        project_q(2, dx)
    query(1)
    ring_take(5, 4)
    for dx in (2, 1, 3, 0):
        project_q(3, dx)
    for i in range(2):
        take(window.at[pl.ds(i * BLOCK, BLOCK)], recv_h.at[i])

    key_row = (y * GROUP + half * BLOCK - GROUP + iota((1, WINDOW), 1)).astype(F32)

    def attend(head):
        logits = dot(queries[head], window[:, 0:HD], ((1,), (1,))) * SCALE
        allowed = (key_row >= opening) & (key_row <= row)
        weight = jnp.where(allowed, jnp.exp(logits), 0.0)
        probs = (weight / jnp.sum(weight, axis=1, keepdims=True)).astype(BF16)
        attended[pl.ds(0, BLOCK), :] = dot(probs, window[:, HD : 2 * HD], ((1,), (0,)))
        product = dot(heads[:, head * HD : (head + 1) * HD], attended[...], ((1,), (1,)), HIGHEST)
        if head == 0:
            part[...] = product
        else:
            part[...] += product

    attend(0)
    attend(1)
    query(2)
    attend(2)

    ends = closing_column(lens)

    def end_of(line, base):
        now = (base + iota((1, LANES), 1)).astype(F32)
        return now, jnp.min(jnp.where(line > now, line, 1e9), axis=0, keepdims=True)

    begin = y * GROUP + half * BLOCK
    now, closing = end_of(jnp.where(micro == 0, ends[:, 0:1], ends[:, 1:2]), begin)
    limit = jnp.minimum(closing, (begin + BLOCK).astype(F32))
    given = y * GROUP + (x // 2) * BLOCK
    carries = []
    for m in range(2):
        there, finish = end_of(ends[:, m : m + 1], given)
        edge = (given + BLOCK).astype(F32)
        decay = jnp.exp(jnp.maximum(edge - 1.0 - there, 0.0) * LOG_LAMBDA)
        decay = jnp.where((finish > edge) & (there < edge), decay, 0.0)
        line = ends[:, m : m + 1]
        beyond = jnp.min(jnp.where(line > edge, line, 1e9), axis=0, keepdims=True)
        through = jnp.where(beyond > edge + BLOCK, LAMBDA_GAE ** (BLOCK - 1), 0.0)
        carries.append((decay, through))

    query(3)
    attend(3)

    rows = [part[k : k + 1, i * HD : (i + 1) * HD] for k in range(2) for i in range(3)]
    tile[...] = jnp.concatenate(rows + [jnp.zeros((2, HD), F32)], axis=0)
    for dz in range(1, NZ):
        remote(tile, terms.at[dz - 1], send_t, recv_t, over_z(dz))
    take(terms, recv_t)
    total = tile[...]
    for i in range(NZ - 1):
        total = total + terms[i]

    value, reward = chain(total[0:3]), chain(total[3:6])
    after = pltpu.roll(value, LANES - 1, 1)
    run = jnp.where(closing == now + 1.0, reward, 0.0) + jnp.where(now + 1.0 < limit, after, 0.0) - value
    for j in range(9):
        step = 2**j
        after = pltpu.roll(run, LANES - step, 1)
        run = run + jnp.where(now + step < limit, LAMBDA_GAE**step * after, 0.0)
    scanned = [total[0:3]] + [run[:, i * HD : (i + 1) * HD] for i in range(3)]
    scanned = jnp.concatenate(scanned + [jnp.zeros((2, HD), F32)], axis=0)
    results[...] = jnp.where(s == 0, total, scanned)

    def deliver(target, core, xc, yc, sem, recv, may_stay):
        if may_stay:
            here = (xc == x) & (yc == y)

            @pl.when(here)
            def _():
                local(results, target, recv)

            @pl.when(jnp.logical_not(here))
            def _():
                remote(results, target, sem, recv, at(core, xc, yc, z))

        else:
            remote(results, target, sem, recv, at(core, xc, yc, z))

    def settle(xc, yc, sem, may_stay):
        if may_stay:

            @pl.when(jnp.logical_not((xc == x) & (yc == y)))
            def _():
                take(results, sem)

        else:
            take(results, sem)

    @pl.when(s == 0)
    def _():
        for i in range(4):
            core, xc = i // 2, 2 * half + i % 2
            deliver(scores.at[micro], core, xc, y, send_g.at[i], recv_p.at[micro], core == 0)

    @pl.when(s == 1)
    def _():
        for k in range(3):
            index = 2 * y + half - k + 2 * NY
            for i in range(4):
                core, xc, yc = i // 2, 2 * (index % 2) + i % 2, (index // 2) % NY
                deliver(
                    blocks.at[micro, k], core, xc, yc, send_g.at[4 * k + i], recv_g.at[micro, k], k < 2 and core == 1
                )

    def outgoing(line):
        return jnp.where(half == 0, line[:, 0:ROWS], line[:, ROWS : 2 * ROWS])

    for m in range(2):
        take(scores.at[m], recv_p.at[m])
        for k in range(3):
            take(blocks.at[m, k], recv_g.at[m, k])
        decay, through = carries[m]
        third = blocks[m, 2, 0:1, 0:1] + LAMBDA_GAE * blocks[m, 2, 3:4, 0:1]
        following = blocks[m, 1, 3:4, 0:1] + through * third
        carry = blocks[m, 1, 0:1, 0:1] + LAMBDA_GAE * following
        value = chain(blocks[m, 0, 0:3])
        advantage = chain(blocks[m, 0, 3:6]) + decay * carry
        out[m : m + 1, :] = outgoing(chain(scores[m, 0:3]))
        out[2 + m : 3 + m, :] = outgoing(advantage)
        out[4 + m : 5 + m, :] = outgoing(advantage + value)

    take(quarters(quarter), send_d)
    for d, dx in ((0, 1), (1, NX - 1)):
        take(raw.at[0, NX - dx], send_a.at[d])
    take(scales.at[pl.ds(1, 7)], send_s)
    for n, (dz, i) in enumerate(spread):
        take(quarters(quarter, i), send_z.at[n])
    for p in range(PIECES):
        for step in range(1, 5):
            ring_take(p, step, send_b)
    for dx in range(3):
        take(raw.at[1, dx + 1], send_c.at[dx])
        take(out_kv.at[dx], send_kv.at[dx])
        for head in range(4):
            take(out_q.at[head, dx], send_q.at[head, dx])
    for i in range(2):
        take(window.at[pl.ds(i * BLOCK, BLOCK)], send_h.at[i])
    take(terms, send_t)

    @pl.when(s == 0)
    def _():
        for i in range(4):
            settle(2 * half + i % 2, y, send_g.at[i], i // 2 == 0)

    @pl.when(s == 1)
    def _():
        for k in range(3):
            index = 2 * y + half - k + 2 * NY
            for i in range(4):
                settle(2 * (index % 2) + i % 2, (index // 2) % NY, send_g.at[4 * k + i], k < 2 and i // 2 == 1)


def split_kernel(lines, scores_out, adv_out, ret_out):
    scores_out[...] = lines[0:2]
    adv_out[...] = lines[2:4]
    ret_out[...] = lines[4:6]


def on_device(hidden, norm_gain, query_weight, keyvalue_weight, policy_head, critic_heads, lengths):
    hbm = pl.BlockSpec(memory_space=pl.ANY)
    dma = pltpu.SemaphoreType.DMA
    vmem = pltpu.VMEM
    lines = pl.pallas_call(
        section_kernel,
        out_shape=jax.ShapeDtypeStruct((8, ROWS), F32),
        in_specs=[hbm] * 7,
        out_specs=pl.BlockSpec(memory_space=pltpu.VMEM),
        scratch_shapes=[
            vmem((ROWS, WIDTH), BF16),
            vmem((2, NX, NY, ROWS, PIECE), BF16),
            vmem((2 * GROUP, NY * PIECE), BF16),
            vmem((3, NY * PIECE, PIECE), BF16),
            vmem((8, 8, ROWS), F32),
            vmem((1, WIDTH), F32),
            vmem((1, 4 * HD), F32),
            vmem((2, 4 * HD), F32),
            vmem((2, NRESP), jnp.int32),
            vmem((BLOCK, PIECE), F32),
            vmem((4, BLOCK, HD), F32),
            vmem((3, BLOCK, PIECE), BF16),
            vmem((3, BLOCK, PIECE), BF16),
            vmem((4, 3, BLOCK, HD), BF16),
            vmem((4, 3, BLOCK, HD), BF16),
            vmem((4, BLOCK, HD), BF16),
            vmem((WINDOW, PIECE), BF16),
            vmem((LANES, HD), F32),
            vmem((8, LANES), F32),
            vmem((8, HD), F32),
            vmem((NZ - 1, 8, HD), F32),
            vmem((8, HD), F32),
            vmem((2, 3, 8, HD), F32),
            vmem((2, 8, HD), F32),
            dma((10,)), dma((2,)), dma((2,)), dma, dma, dma((4,)), dma((4,)), dma((3,)), dma((3,)), dma, dma,
            dma((PIECES, 4, 2)), dma((PIECES, 4, 2)), dma((3,)), dma((3,)), dma((4, 3)), dma((4, 3)),
            dma((2,)), dma((2,)), dma, dma, dma((12,)), dma((2, 3)), dma((2,)),
        ],
        compiler_params=pltpu.CompilerParams(
            collective_id=0, has_side_effects=True, vmem_limit_bytes=60 * 1024 * 1024
        ),
        name="section",
    )(
        hidden,
        norm_gain,
        query_weight[0],
        keyvalue_weight[0].reshape(PIECE, 2 * HD),
        policy_head.reshape(1, -1),
        critic_heads,
        lengths,
    )
    line = jax.ShapeDtypeStruct((2, ROWS), F32)
    return pl.pallas_call(split_kernel, out_shape=(line, line, line), name="split")(lines)


def solution(mesh):
    placed = (
        P(None, "seq", None),
        P("sec", None),
        P("sec", "seq", "mp"),
        P("sec", "seq", None, "mp"),
        P("mp"),
        P(None, "mp"),
        P(),
    )
    return jax.shard_map(
        on_device,
        mesh=mesh,
        in_specs=placed,
        out_specs=(P(None, "seq"), P(None, "seq"), P(None, "seq")),
        check_vma=False,
    )
```

```python
import functools

import jax
import jax.numpy as jnp
from jax import lax
from jax.experimental import pallas as pl
from jax.experimental.pallas import tpu as pltpu
from jax.sharding import PartitionSpec as P

F32 = jnp.float32
BF16 = jnp.bfloat16
MESH = pl.DeviceIdType.MESH
HIGHEST = lax.Precision.HIGHEST

HD = 128
NX, NY, NZ = 4, 8, 8
ROWS = 144
BLOCK = 288
GROUP = 576
WINDOW = 864
WIDTH = 8192
PIECE = 256
NRESP = 64
LANES = 384
PIECES = 6
LAMBDA_GAE = 0.95
LOG_LAMBDA = -0.05129329438755058
LOG_BASE = 13.815510557964274
NORM_EPS = 1e-06
SCALE = float(HD) ** -0.5

REL = (0, 1, -1, 2, -2, 3, -3, 4)
PLACE = {0: 0, 1: 1, -1: 2, 2: 3, -2: 4, 3: 5, -3: 6, 4: 7, -4: 7}


def rel_of(place):
    return ((place + 1) // 2) * (2 * (place % 2) - 1)


def remote(src, dst, send, recv, device):
    copy = pltpu.make_async_remote_copy(
        src_ref=src, dst_ref=dst, send_sem=send, recv_sem=recv, device_id=device, device_id_type=MESH
    )
    copy.start()


def local(src, dst, sem):
    pltpu.make_async_copy(src, dst, sem).start()


def take(ref, sem):
    pltpu.make_async_copy(ref, ref, sem).wait()


def iota(shape, axis):
    return lax.broadcasted_iota(jnp.int32, shape, axis)


def dot(a, b, over, precision=None):
    return lax.dot_general(
        a, b, ((over[0], over[1]), ((), ())), precision=precision, preferred_element_type=F32
    )


def chain(refs):
    return jnp.concatenate([refs[i : i + 1] for i in range(3)], axis=1)


def closing_row(lengths):
    upto = (iota((NRESP, NRESP), 0) <= iota((NRESP, NRESP), 1)).astype(F32)
    return dot(lengths, upto, ((1,), (0,)), HIGHEST)


def closing_column(lengths):
    upto = (iota((NRESP, NRESP), 1) <= iota((NRESP, NRESP), 0)).astype(F32)
    return dot(upto, lengths, ((1,), (1,)), HIGHEST)


def places():
    s = lax.axis_index("sec")
    q = lax.axis_index("seq")
    z = lax.axis_index("mp")
    return s, q % NX, q // NX, z


def at(s, x, y, z):
    return (s, y * NX + x, z)


def section_kernel(
    hid, gain_hbm, qw, kvw, policy_hbm, critic_hbm, lengths_hbm, out,
    hbuf, raw, normed, pairs, wts, scales, gain, policy, critic, lengths,
    own_kv, own_q, out_kv, in_kv, out_q, in_q, queries, window, attended, part, tile, terms, results, blocks, scores,
    sem_loc, send_a, recv_a, send_d, recv_d, send_z, recv_z, send_c, recv_c, send_s, recv_s, send_b, recv_b,
    send_kv, recv_kv, send_q, recv_q, send_h, recv_h, send_t, recv_t, send_g, recv_g, recv_p,
):
    s, x, y, z = places()
    micro, half = x // 2, x % 2
    other = 1 - s

    def chip(dx=0, dy=0, core=None):
        return at(s if core is None else core, (x + dx) % NX, (y + dy + NY) % NY, z)

    def over_z(dz):
        return at(s, x, y, (z + dz + NZ) % NZ)

    sibling = at(other, x, y, z)
    barrier = pltpu.get_barrier_semaphore()
    partners = [chip(dx, 0, (s + ds) % 2) for ds in range(2) for dx in range(NX)][1:]
    partners = partners + [chip(dx, dy, core) for core in range(2) for dx in range(NX) for dy in (-1, 1)]
    partners = partners + [over_z(dz) for dz in range(1, NZ)]
    for device in partners:
        pl.semaphore_signal(barrier, inc=1, device_id=device, device_id_type=MESH)
    def column(place, xx):
        start = ((y + rel_of(place) + NY) % NY) * (NX * PIECE) + xx * PIECE
        return pl.ds(pl.multiple_of(start, PIECE), PIECE)

    local(hid.at[s], hbuf, sem_loc.at[0])
    local(kvw, pairs, sem_loc.at[7])
    local(gain_hbm, gain, sem_loc.at[1])
    local(policy_hbm, policy, sem_loc.at[2])
    local(critic_hbm, critic, sem_loc.at[3])
    local(lengths_hbm, lengths, sem_loc.at[4])
    for place in range(NY):
        local(hid.at[s, :, column(place, x)], raw.at[0, 0, place], sem_loc.at[5])
        local(hid.at[other, :, column(place, x)], raw.at[1, 0, place], sem_loc.at[6])
    for i in range(2):
        local(qw.at[:, pl.ds(i * PIECE, PIECE)], wts.at[i + 1, pl.ds(0, PIECE)], sem_loc.at[8 + i])

    take(hbuf, sem_loc.at[0])

    def squares(i, total):
        for j in range(4):
            start = pl.multiple_of((i * 4 + j) * HD, HD)
            block = hbuf[:, pl.ds(start, HD)].astype(F32)
            total = total + block * block
        return total

    total = lax.fori_loop(0, WIDTH // HD // 4, squares, jnp.zeros((ROWS, HD), F32))
    mean = dot(jnp.ones((8, HD), F32), total, ((1,), (1,)), HIGHEST) * (1.0 / WIDTH)
    scales[0] = lax.rsqrt(mean + NORM_EPS)
    take(pairs, sem_loc.at[7])
    for i in range(2):
        chosen = iota((PIECE, 2 * PIECE), 1) == 2 * iota((PIECE, 2 * PIECE), 0) + i
        sorted_rows = dot(chosen.astype(F32).astype(BF16), pairs[...], ((1,), (0,)))
        wts[0, 0:PIECE, i * HD : (i + 1) * HD] = sorted_rows.astype(BF16)

    pl.semaphore_wait(barrier, len(partners))

    def weights(p, place, piece=None):
        begin, size = place * PIECE, PIECE
        if piece is not None:
            begin, size = begin + piece * (PIECE // 2), PIECE // 2
        return wts.at[p // 2, pl.ds(begin, size), pl.ds((p % 2) * HD, HD)]

    def mine(p):
        return weights(p, 0) if p < 2 else qw.at[:, pl.ds((p - 2) * HD, HD)]

    ring_y = [chip(0, 1), chip(0, -1)]

    def ring_send(p, step, ways=(0, 1)):
        for d in ways:
            sign, piece = 1 - 2 * d, d if step == 4 else None
            target = weights(p, PLACE[-sign * step], piece)
            source = mine(p) if step == 1 else weights(p, PLACE[-sign * (step - 1)], piece)
            remote(source, target, send_b.at[p, step - 1, d], recv_b.at[p, step - 1, d], ring_y[d])

    def ring_take(p, step, sems=None, ways=(0, 1)):
        sems = recv_b if sems is None else sems
        for d in ways:
            sign, piece = 1 - 2 * d, d if step == 4 else None
            take(weights(p, PLACE[-sign * step], piece), sems.at[p, step - 1, d])

    def ring(p, step):
        for d in range(2):
            ring_take(p, step, None, (d,))
            ring_send(p, step + 1, (d,))

    def to_neighbours(place):
        for d, dx in ((0, 1), (1, NX - 1)):
            remote(
                hid.at[s, :, column(place, (x + dx) % NX)],
                raw.at[0, NX - dx, place],
                send_a.at[d],
                recv_a.at[d],
                chip(dx),
            )

    for p in range(3):
        ring_send(p, 1)
    facing = (x + 2) % NX
    quarter = z % 4
    for i in range(2):
        remote(
            hid.at[s, :, column(2 * quarter + i, facing)], raw.at[0, 2, 2 * quarter + i], send_d, recv_d, chip(2)
        )
    for ds in range(2):
        for dx in range(NX):
            if ds + dx > 0:
                slot = ((2 - ds) % 2) * NX + (NX - dx) % NX
                remote(scales.at[0], scales.at[slot], send_s, recv_s, chip(dx, 0, (s + ds) % 2))
    def quarters(t, i=None):
        begin = 2 * ((t + 4) % 4)
        return raw.at[0, 2, pl.ds(begin, 2)] if i is None else raw.at[0, 2, begin + i]

    spread = ((1, None), (-1, None), (2, 1), (-2, 0))
    for place in range(NY):
        to_neighbours(place)

    ring(0, 1)
    ring(1, 1)
    take(quarters(quarter), recv_d)
    for n, (dz, i) in enumerate(spread):
        remote(quarters(quarter, i), quarters(quarter, i), send_z.at[n], recv_z.at[n], over_z(dz))
    ring(2, 1)

    take(lengths, sem_loc.at[4])
    lens = lengths[...].astype(F32)
    openings = closing_row(lens) - lens
    opening_line = jnp.where(micro == 0, openings[0:1], openings[1:2])
    row = (y * GROUP + half * BLOCK + iota((BLOCK, 1), 0)).astype(F32)
    opening = jnp.max(jnp.where(opening_line <= row, opening_line, 0.0), axis=1, keepdims=True)
    lane = iota((1, HD), 1)
    inverse = jnp.exp((lane % (HD // 2)).astype(F32) * (-2.0 * LOG_BASE / HD))
    angle = (row - opening) * inverse
    cosine = jnp.cos(angle)
    sine = jnp.sin(angle) * jnp.where(lane < HD // 2, -1.0, 1.0)

    def rotated(v):
        return (v * cosine + pltpu.roll(v, HD // 2, 1) * sine).astype(BF16)

    ends = closing_column(lens)

    def end_of(line, base):
        now = (base + iota((1, LANES), 1)).astype(F32)
        return now, jnp.min(jnp.where(line > now, line, 1e9), axis=0, keepdims=True)

    begin = y * GROUP + half * BLOCK
    now, closing = end_of(jnp.where(micro == 0, ends[:, 0:1], ends[:, 1:2]), begin)
    limit = jnp.minimum(closing, (begin + BLOCK).astype(F32))
    given = y * GROUP + (x // 2) * BLOCK
    carries = []
    for m in range(2):
        there, finish = end_of(ends[:, m : m + 1], given)
        edge = (given + BLOCK).astype(F32)
        decay = jnp.exp(jnp.maximum(edge - 1.0 - there, 0.0) * LOG_LAMBDA)
        decay = jnp.where((finish > edge) & (there < edge), decay, 0.0)
        line = ends[:, m : m + 1]
        beyond = jnp.min(jnp.where(line > edge, line, 1e9), axis=0, keepdims=True)
        through = jnp.where(beyond > edge + BLOCK, LAMBDA_GAE ** (BLOCK - 1), 0.0)
        carries.append((decay, through))

    take(policy, sem_loc.at[2])
    take(critic, sem_loc.at[3])
    kind = iota((8, 4 * HD), 0)
    first = jnp.where(s == 0, policy[...], critic[0:1])
    second = jnp.where(s == 0, 0.0, critic[1:2])
    heads = jnp.where(kind == 0, first, jnp.where(kind == 1, second, 0.0))
    attended[pl.ds(BLOCK, LANES - BLOCK), :] = jnp.zeros((LANES - BLOCK, HD), F32)

    take(scales.at[pl.ds(1, 7)], recv_s)
    take(gain, sem_loc.at[1])

    def normalise(ds, dx):
        base = (((s + ds) % 2) * NX + (x + dx) % NX) * ROWS
        rows = pl.ds(pl.multiple_of(base, 16), ROWS)
        first_row = (iota((8, PIECE), 0) == 0).astype(F32)
        scale = dot(scales[ds * NX + dx], first_row, ((0,), (0,)), HIGHEST)

        def one(place, carry):
            block = raw[ds, dx, place].astype(F32) * scale * gain[0:1, column(place, x)]
            normed[rows, pl.ds(pl.multiple_of(place * PIECE, PIECE), PIECE)] = block.astype(BF16)
            return carry

        lax.fori_loop(0, NY, one, 0)

    def to_sibling(dx):
        remote(raw.at[0, dx], raw.at[1, dx], send_c.at[dx - 1], recv_c.at[dx - 1], sibling)

    def from_sibling(dx):
        take(raw.at[1, dx], recv_c.at[dx - 1])
        normalise(1, dx)

    def rows_of(dx):
        return pl.ds(pl.multiple_of(((x + dx) % NX) * BLOCK, 32), BLOCK)

    def project_kv(dx):
        product = dot(normed[rows_of(dx), :], wts[0], ((1,), (0,)))
        if dx == 0:
            own_kv[...] = product
        else:
            out_kv[dx - 1] = product.astype(BF16)
            remote(out_kv.at[dx - 1], in_kv.at[dx - 1], send_kv.at[dx - 1], recv_kv.at[dx - 1], chip(dx))

    def project_q(head, dx):
        piece = wts[1 + head // 2, :, (head % 2) * HD : (head % 2 + 1) * HD]
        product = dot(normed[rows_of(dx), :], piece, ((1,), (0,)))
        if dx == 0:
            own_q[head] = product
        else:
            out_q[head, dx - 1] = product.astype(BF16)
            remote(
                out_q.at[head, dx - 1],
                in_q.at[head, dx - 1],
                send_q.at[head, dx - 1],
                recv_q.at[head, dx - 1],
                chip(dx),
            )

    def query(head):
        for dx in range(3):
            take(in_q.at[head, dx], recv_q.at[head, dx])
        summed = own_q[head]
        for dx in range(3):
            summed = summed + in_q[head, dx].astype(F32)
        queries[head] = rotated(summed)

    def project(head, order=(2, 1, 3, 0)):
        for dx in order:
            if head is None:
                project_kv(dx)
            else:
                project_q(head, dx)

    def key_value():
        for dx in range(3):
            take(in_kv.at[dx], recv_kv.at[dx])
        keyvalue = own_kv[...]
        for dx in range(3):
            keyvalue = keyvalue + in_kv[dx].astype(F32)
        window[pl.ds(2 * BLOCK, BLOCK), 0:HD] = rotated(keyvalue[:, 0:HD])
        window[pl.ds(2 * BLOCK, BLOCK), HD : 2 * HD] = keyvalue[:, HD : 2 * HD].astype(BF16)
        next_block = at(s, 2 * micro + 1 - half, (y + half) % NY, z)
        for i, device in ((0, chip(0, 1)), (1, next_block)):
            remote(
                window.at[pl.ds(2 * BLOCK, BLOCK)],
                window.at[pl.ds(i * BLOCK, BLOCK)],
                send_h.at[i],
                recv_h.at[i],
                device,
            )

    take(raw.at[0, 0], sem_loc.at[5])
    take(raw.at[1, 0], sem_loc.at[6])
    for i in range(1, 3):
        take(wts.at[i, pl.ds(0, PIECE)], sem_loc.at[7 + i])
    ring(0, 2)
    normalise(0, 0)
    ring(1, 2)
    normalise(1, 0)
    ring(2, 2)
    ring(0, 3)
    ring_send(3, 1)
    ring(1, 3)
    ring_send(4, 1)
    ring(2, 3)
    for n, (dz, i) in enumerate(spread):
        take(quarters(quarter - dz, i), recv_z.at[n])
    to_sibling(2)
    normalise(0, 2)
    ring(3, 1)
    ring_send(5, 1)
    from_sibling(2)
    for d, dx in ((0, 3), (1, 1)):
        take(raw.at[0, dx], recv_a.at[d])
        to_sibling(dx)
    ring(4, 1)
    normalise(0, 3)
    normalise(0, 1)
    from_sibling(3)
    from_sibling(1)
    ring_take(0, 4)
    ring_take(1, 4)
    ring(3, 2)
    project(None, (2, 1))
    ring(5, 1)
    project(None, (3, 0))
    ring(4, 2)
    ring_take(2, 4)
    project(0)
    ring(3, 3)
    ring(5, 2)
    ring(4, 3)
    ring_take(3, 4)
    project(1)
    key_value()
    ring(5, 3)
    ring_take(4, 4)
    project(2)
    query(0)
    ring_take(5, 4)
    project(3)
    query(1)
    for i in range(2):
        take(window.at[pl.ds(i * BLOCK, BLOCK)], recv_h.at[i])

    key_row = (y * GROUP + half * BLOCK - GROUP + iota((1, WINDOW), 1)).astype(F32)

    def attend(head):
        logits = dot(queries[head], window[:, 0:HD], ((1,), (1,))) * SCALE
        allowed = (key_row >= opening) & (key_row <= row)
        weight = jnp.where(allowed, jnp.exp(logits), 0.0)
        probs = (weight / jnp.sum(weight, axis=1, keepdims=True)).astype(BF16)
        attended[pl.ds(0, BLOCK), :] = dot(probs, window[:, HD : 2 * HD], ((1,), (0,)))
        product = dot(heads[:, head * HD : (head + 1) * HD], attended[...], ((1,), (1,)), HIGHEST)
        if head == 0:
            part[...] = product
        else:
            part[...] += product

    attend(0)
    attend(1)
    query(2)
    attend(2)

    query(3)
    attend(3)

    rows = [part[k : k + 1, i * HD : (i + 1) * HD] for k in range(2) for i in range(3)]
    tile[...] = jnp.concatenate(rows + [jnp.zeros((2, HD), F32)], axis=0)
    for dz in range(1, NZ):
        remote(tile, terms.at[dz - 1], send_t, recv_t, over_z(dz))
    take(terms, recv_t)
    total = tile[...]
    for i in range(NZ - 1):
        total = total + terms[i]

    value, reward = chain(total[0:3]), chain(total[3:6])
    after = pltpu.roll(value, LANES - 1, 1)
    run = jnp.where(closing == now + 1.0, reward, 0.0) + jnp.where(now + 1.0 < limit, after, 0.0) - value
    for j in range(9):
        step = 2**j
        after = pltpu.roll(run, LANES - step, 1)
        run = run + jnp.where(now + step < limit, LAMBDA_GAE**step * after, 0.0)
    scanned = [total[0:3]] + [run[:, i * HD : (i + 1) * HD] for i in range(3)]
    scanned = jnp.concatenate(scanned + [jnp.zeros((2, HD), F32)], axis=0)
    results[...] = jnp.where(s == 0, total, scanned)

    def deliver(target, core, xc, yc, sem, recv, may_stay):
        if may_stay:
            here = (xc == x) & (yc == y)

            @pl.when(here)
            def _():
                local(results, target, recv)

            @pl.when(jnp.logical_not(here))
            def _():
                remote(results, target, sem, recv, at(core, xc, yc, z))

        else:
            remote(results, target, sem, recv, at(core, xc, yc, z))

    def settle(xc, yc, sem, may_stay):
        if may_stay:

            @pl.when(jnp.logical_not((xc == x) & (yc == y)))
            def _():
                take(results, sem)

        else:
            take(results, sem)

    @pl.when(s == 0)
    def _():
        for i in range(4):
            core, xc = i // 2, 2 * half + i % 2
            deliver(scores.at[micro], core, xc, y, send_g.at[i], recv_p.at[micro], core == 0)

    @pl.when(s == 1)
    def _():
        for k in range(3):
            index = 2 * y + half - k + 2 * NY
            for i in range(4):
                core, xc, yc = i // 2, 2 * (index % 2) + i % 2, (index // 2) % NY
                deliver(
                    blocks.at[micro, k], core, xc, yc, send_g.at[4 * k + i], recv_g.at[micro, k], k < 2 and core == 1
                )

    def outgoing(line):
        return jnp.where(half == 0, line[:, 0:ROWS], line[:, ROWS : 2 * ROWS])

    for m in range(2):
        take(scores.at[m], recv_p.at[m])
        for k in range(3):
            take(blocks.at[m, k], recv_g.at[m, k])
        decay, through = carries[m]
        third = blocks[m, 2, 0:1, 0:1] + LAMBDA_GAE * blocks[m, 2, 3:4, 0:1]
        following = blocks[m, 1, 3:4, 0:1] + through * third
        carry = blocks[m, 1, 0:1, 0:1] + LAMBDA_GAE * following
        value = chain(blocks[m, 0, 0:3])
        advantage = chain(blocks[m, 0, 3:6]) + decay * carry
        out[m : m + 1, :] = outgoing(chain(scores[m, 0:3]))
        out[2 + m : 3 + m, :] = outgoing(advantage)
        out[4 + m : 5 + m, :] = outgoing(advantage + value)

    take(quarters(quarter), send_d)
    for d, dx in ((0, 1), (1, NX - 1)):
        take(raw.at[0, NX - dx], send_a.at[d])
    take(scales.at[pl.ds(1, 7)], send_s)
    for n, (dz, i) in enumerate(spread):
        take(quarters(quarter, i), send_z.at[n])
    for p in range(PIECES):
        for step in range(1, 5):
            ring_take(p, step, send_b)
    for dx in range(3):
        take(raw.at[1, dx + 1], send_c.at[dx])
        take(out_kv.at[dx], send_kv.at[dx])
        for head in range(4):
            take(out_q.at[head, dx], send_q.at[head, dx])
    for i in range(2):
        take(window.at[pl.ds(i * BLOCK, BLOCK)], send_h.at[i])
    take(terms, send_t)

    @pl.when(s == 0)
    def _():
        for i in range(4):
            settle(2 * half + i % 2, y, send_g.at[i], i // 2 == 0)

    @pl.when(s == 1)
    def _():
        for k in range(3):
            index = 2 * y + half - k + 2 * NY
            for i in range(4):
                settle(2 * (index % 2) + i % 2, (index // 2) % NY, send_g.at[4 * k + i], k < 2 and i // 2 == 1)


def split_kernel(lines, scores_out, adv_out, ret_out):
    scores_out[...] = lines[0:2]
    adv_out[...] = lines[2:4]
    ret_out[...] = lines[4:6]


def on_device(hidden, norm_gain, query_weight, keyvalue_weight, policy_head, critic_heads, lengths):
    hbm = pl.BlockSpec(memory_space=pl.ANY)
    dma = pltpu.SemaphoreType.DMA
    vmem = pltpu.VMEM
    lines = pl.pallas_call(
        section_kernel,
        out_shape=jax.ShapeDtypeStruct((8, ROWS), F32),
        in_specs=[hbm] * 7,
        out_specs=pl.BlockSpec(memory_space=pltpu.VMEM),
        scratch_shapes=[
            vmem((ROWS, WIDTH), BF16),
            vmem((2, NX, NY, ROWS, PIECE), BF16),
            vmem((2 * GROUP, NY * PIECE), BF16),
            vmem((2 * PIECE, HD), BF16),
            vmem((3, NY * PIECE, PIECE), BF16),
            vmem((8, 8, ROWS), F32),
            vmem((1, WIDTH), F32),
            vmem((1, 4 * HD), F32),
            vmem((2, 4 * HD), F32),
            vmem((2, NRESP), jnp.int32),
            vmem((BLOCK, PIECE), F32),
            vmem((4, BLOCK, HD), F32),
            vmem((3, BLOCK, PIECE), BF16),
            vmem((3, BLOCK, PIECE), BF16),
            vmem((4, 3, BLOCK, HD), BF16),
            vmem((4, 3, BLOCK, HD), BF16),
            vmem((4, BLOCK, HD), BF16),
            vmem((WINDOW, PIECE), BF16),
            vmem((LANES, HD), F32),
            vmem((8, LANES), F32),
            vmem((8, HD), F32),
            vmem((NZ - 1, 8, HD), F32),
            vmem((8, HD), F32),
            vmem((2, 3, 8, HD), F32),
            vmem((2, 8, HD), F32),
            dma((10,)), dma((2,)), dma((2,)), dma, dma, dma((4,)), dma((4,)), dma((3,)), dma((3,)), dma, dma,
            dma((PIECES, 4, 2)), dma((PIECES, 4, 2)), dma((3,)), dma((3,)), dma((4, 3)), dma((4, 3)),
            dma((2,)), dma((2,)), dma, dma, dma((12,)), dma((2, 3)), dma((2,)),
        ],
        compiler_params=pltpu.CompilerParams(
            collective_id=0, has_side_effects=True, vmem_limit_bytes=60 * 1024 * 1024
        ),
        name="section",
    )(
        hidden,
        norm_gain,
        query_weight[0],
        keyvalue_weight.reshape(2 * PIECE, HD),
        policy_head.reshape(1, -1),
        critic_heads,
        lengths,
    )
    line = jax.ShapeDtypeStruct((2, ROWS), F32)
    return pl.pallas_call(split_kernel, out_shape=(line, line, line), name="split")(lines)


def solution(mesh):
    placed = (
        P(None, "seq", None),
        P("sec", None),
        P("sec", "seq", "mp"),
        P("sec", "seq", None, "mp"),
        P("mp"),
        P(None, "mp"),
        P(),
    )
    return jax.shard_map(
        on_device,
        mesh=mesh,
        in_specs=placed,
        out_specs=(P(None, "seq"), P(None, "seq"), P(None, "seq")),
        check_vma=False,
    )
```

```python
import functools

import jax
import jax.numpy as jnp
from jax import lax
from jax.experimental import pallas as pl
from jax.experimental.pallas import tpu as pltpu
from jax.sharding import PartitionSpec as P

F32 = jnp.float32
BF16 = jnp.bfloat16
MESH = pl.DeviceIdType.MESH
HIGHEST = lax.Precision.HIGHEST

HD = 128
NX, NY, NZ = 4, 8, 8
ROWS = 144
BLOCK = 288
GROUP = 576
WINDOW = 864
WIDTH = 8192
PIECE = 256
NRESP = 64
LANES = 384
PIECES = 6
LAMBDA_GAE = 0.95
LOG_LAMBDA = -0.05129329438755058
LOG_BASE = 13.815510557964274
NORM_EPS = 1e-06
SCALE = float(HD) ** -0.5

REL = (0, 1, -1, 2, -2, 3, -3, 4)
PLACE = {0: 0, 1: 1, -1: 2, 2: 3, -2: 4, 3: 5, -3: 6, 4: 7, -4: 7}


def rel_of(place):
    return ((place + 1) // 2) * (2 * (place % 2) - 1)


def remote(src, dst, send, recv, device):
    copy = pltpu.make_async_remote_copy(
        src_ref=src, dst_ref=dst, send_sem=send, recv_sem=recv, device_id=device, device_id_type=MESH
    )
    copy.start()


def local(src, dst, sem):
    pltpu.make_async_copy(src, dst, sem).start()


def take(ref, sem):
    pltpu.make_async_copy(ref, ref, sem).wait()


def iota(shape, axis):
    return lax.broadcasted_iota(jnp.int32, shape, axis)


def dot(a, b, over, precision=None):
    return lax.dot_general(
        a, b, ((over[0], over[1]), ((), ())), precision=precision, preferred_element_type=F32
    )


def chain(refs):
    return jnp.concatenate([refs[i : i + 1] for i in range(3)], axis=1)


def closing_row(lengths):
    upto = (iota((NRESP, NRESP), 0) <= iota((NRESP, NRESP), 1)).astype(F32)
    return dot(lengths, upto, ((1,), (0,)), HIGHEST)


def closing_column(lengths):
    upto = (iota((NRESP, NRESP), 1) <= iota((NRESP, NRESP), 0)).astype(F32)
    return dot(upto, lengths, ((1,), (1,)), HIGHEST)


def places():
    s = lax.axis_index("sec")
    q = lax.axis_index("seq")
    z = lax.axis_index("mp")
    return s, q % NX, q // NX, z


def at(s, x, y, z):
    return (s, y * NX + x, z)


def section_kernel(
    hid, gain_hbm, qw, kvw, policy_hbm, critic_hbm, lengths_hbm, out,
    hbuf, raw, normed, pairs, wts, scales, gain, policy, critic, lengths,
    own_kv, own_q, out_kv, in_kv, out_q, in_q, queries, window, attended, part, tile, terms, results, blocks, scores,
    sem_loc, send_a, recv_a, send_d, recv_d, send_z, recv_z, send_c, recv_c, send_s, recv_s, send_b, recv_b,
    send_kv, recv_kv, send_q, recv_q, send_h, recv_h, send_t, recv_t, send_g, recv_g, recv_p,
):
    s, x, y, z = places()
    micro, half = x // 2, x % 2
    other = 1 - s

    def chip(dx=0, dy=0, core=None):
        return at(s if core is None else core, (x + dx) % NX, (y + dy + NY) % NY, z)

    def over_z(dz):
        return at(s, x, y, (z + dz + NZ) % NZ)

    sibling = at(other, x, y, z)
    barrier = pltpu.get_barrier_semaphore()
    partners = [chip(dx, 0, (s + ds) % 2) for ds in range(2) for dx in range(NX)][1:]
    partners = partners + [chip(dx, dy, core) for core in range(2) for dx in range(NX) for dy in (-1, 1)]
    partners = partners + [over_z(dz) for dz in range(1, NZ)]
    for device in partners:
        pl.semaphore_signal(barrier, inc=1, device_id=device, device_id_type=MESH)
    def column(place, xx):
        start = ((y + rel_of(place) + NY) % NY) * (NX * PIECE) + xx * PIECE
        return pl.ds(pl.multiple_of(start, PIECE), PIECE)

    local(hid.at[s], hbuf, sem_loc.at[0])
    local(kvw, pairs, sem_loc.at[7])
    local(gain_hbm, gain, sem_loc.at[1])
    local(policy_hbm, policy, sem_loc.at[2])
    local(critic_hbm, critic, sem_loc.at[3])
    local(lengths_hbm, lengths, sem_loc.at[4])
    for place in range(NY):
        local(hid.at[s, :, column(place, x)], raw.at[0, 0, place], sem_loc.at[5])
        local(hid.at[other, :, column(place, x)], raw.at[1, 0, place], sem_loc.at[6])
    for i in range(2):
        local(qw.at[:, pl.ds(i * PIECE, PIECE)], wts.at[i + 1, pl.ds(0, PIECE)], sem_loc.at[8 + i])

    take(hbuf, sem_loc.at[0])

    def squares(i, total):
        for j in range(4):
            start = pl.multiple_of((i * 4 + j) * HD, HD)
            block = hbuf[:, pl.ds(start, HD)].astype(F32)
            total = total + block * block
        return total

    total = lax.fori_loop(0, WIDTH // HD // 4, squares, jnp.zeros((ROWS, HD), F32))
    mean = dot(jnp.ones((8, HD), F32), total, ((1,), (1,)), HIGHEST) * (1.0 / WIDTH)
    scales[0] = lax.rsqrt(mean + NORM_EPS)
    take(pairs, sem_loc.at[7])
    for i in range(2):
        chosen = iota((PIECE, 2 * PIECE), 1) == 2 * iota((PIECE, 2 * PIECE), 0) + i
        sorted_rows = dot(chosen.astype(F32).astype(BF16), pairs[...], ((1,), (0,)))
        wts[0, 0:PIECE, i * HD : (i + 1) * HD] = sorted_rows.astype(BF16)

    pl.semaphore_wait(barrier, len(partners))

    def weights(p, place, piece=None):
        begin, size = place * PIECE, PIECE
        if piece is not None:
            begin, size = begin + piece * (PIECE // 2), PIECE // 2
        return wts.at[p // 2, pl.ds(begin, size), pl.ds((p % 2) * HD, HD)]

    def mine(p):
        return weights(p, 0) if p < 2 else qw.at[:, pl.ds((p - 2) * HD, HD)]

    ring_y = [chip(0, 1), chip(0, -1)]

    def ring_send(p, step, ways=(0, 1)):
        for d in ways:
            sign, piece = 1 - 2 * d, d if step == 4 else None
            target = weights(p, PLACE[-sign * step], piece)
            source = mine(p) if step == 1 else weights(p, PLACE[-sign * (step - 1)], piece)
            remote(source, target, send_b.at[p, step - 1, d], recv_b.at[p, step - 1, d], ring_y[d])

    def ring_take(p, step, sems=None, ways=(0, 1)):
        sems = recv_b if sems is None else sems
        for d in ways:
            sign, piece = 1 - 2 * d, d if step == 4 else None
            take(weights(p, PLACE[-sign * step], piece), sems.at[p, step - 1, d])

    def ring(p, step):
        for d in range(2):
            ring_take(p, step, None, (d,))
            ring_send(p, step + 1, (d,))

    def to_neighbours(place):
        for d, dx in ((0, 1), (1, NX - 1)):
            remote(
                hid.at[s, :, column(place, (x + dx) % NX)],
                raw.at[0, NX - dx, place],
                send_a.at[d],
                recv_a.at[d],
                chip(dx),
            )

    for p in range(3):
        ring_send(p, 1)
    facing = (x + 2) % NX
    quarter = z % 4
    for i in range(2):
        remote(
            hid.at[s, :, column(2 * quarter + i, facing)], raw.at[0, 2, 2 * quarter + i], send_d, recv_d, chip(2)
        )
    for ds in range(2):
        for dx in range(NX):
            if ds + dx > 0:
                slot = ((2 - ds) % 2) * NX + (NX - dx) % NX
                remote(scales.at[0], scales.at[slot], send_s, recv_s, chip(dx, 0, (s + ds) % 2))
    def quarters(t, i=None):
        begin = 2 * ((t + 4) % 4)
        return raw.at[0, 2, pl.ds(begin, 2)] if i is None else raw.at[0, 2, begin + i]

    spread = ((1, None), (-1, None), (2, 1), (-2, 0))
    for place in range(NY):
        to_neighbours(place)

    ring(0, 1)
    ring(1, 1)
    take(quarters(quarter), recv_d)
    for n, (dz, i) in enumerate(spread):
        remote(quarters(quarter, i), quarters(quarter, i), send_z.at[n], recv_z.at[n], over_z(dz))
    ring(2, 1)

    take(lengths, sem_loc.at[4])
    lens = lengths[...].astype(F32)
    openings = closing_row(lens) - lens
    opening_line = jnp.where(micro == 0, openings[0:1], openings[1:2])
    row = (y * GROUP + half * BLOCK + iota((BLOCK, 1), 0)).astype(F32)
    opening = jnp.max(jnp.where(opening_line <= row, opening_line, 0.0), axis=1, keepdims=True)
    lane = iota((1, HD), 1)
    inverse = jnp.exp((lane % (HD // 2)).astype(F32) * (-2.0 * LOG_BASE / HD))
    angle = (row - opening) * inverse
    cosine = jnp.cos(angle)
    sine = jnp.sin(angle) * jnp.where(lane < HD // 2, -1.0, 1.0)

    def rotated(v):
        return (v * cosine + pltpu.roll(v, HD // 2, 1) * sine).astype(BF16)

    ends = closing_column(lens)

    def end_of(line, base):
        now = (base + iota((1, LANES), 1)).astype(F32)
        return now, jnp.min(jnp.where(line > now, line, 1e9), axis=0, keepdims=True)

    begin = y * GROUP + half * BLOCK
    now, closing = end_of(jnp.where(micro == 0, ends[:, 0:1], ends[:, 1:2]), begin)
    limit = jnp.minimum(closing, (begin + BLOCK).astype(F32))
    given = y * GROUP + (x // 2) * BLOCK
    carries = []
    for m in range(2):
        there, finish = end_of(ends[:, m : m + 1], given)
        edge = (given + BLOCK).astype(F32)
        decay = jnp.exp(jnp.maximum(edge - 1.0 - there, 0.0) * LOG_LAMBDA)
        decay = jnp.where((finish > edge) & (there < edge), decay, 0.0)
        line = ends[:, m : m + 1]
        beyond = jnp.min(jnp.where(line > edge, line, 1e9), axis=0, keepdims=True)
        through = jnp.where(beyond > edge + BLOCK, LAMBDA_GAE ** (BLOCK - 1), 0.0)
        carries.append((decay, through))

    take(policy, sem_loc.at[2])
    take(critic, sem_loc.at[3])
    kind = iota((8, 4 * HD), 0)
    first = jnp.where(s == 0, policy[...], critic[0:1])
    second = jnp.where(s == 0, 0.0, critic[1:2])
    heads = jnp.where(kind == 0, first, jnp.where(kind == 1, second, 0.0))
    attended[pl.ds(BLOCK, LANES - BLOCK), :] = jnp.zeros((LANES - BLOCK, HD), F32)

    take(scales.at[pl.ds(1, 7)], recv_s)
    take(gain, sem_loc.at[1])

    def normalise(ds, dx):
        base = (((s + ds) % 2) * NX + (x + dx) % NX) * ROWS
        rows = pl.ds(pl.multiple_of(base, 16), ROWS)
        first_row = (iota((8, PIECE), 0) == 0).astype(F32)
        scale = dot(scales[ds * NX + dx], first_row, ((0,), (0,)), HIGHEST)

        def one(place, carry):
            block = raw[ds, dx, place].astype(F32) * scale * gain[0:1, column(place, x)]
            normed[rows, pl.ds(pl.multiple_of(place * PIECE, PIECE), PIECE)] = block.astype(BF16)
            return carry

        lax.fori_loop(0, NY, one, 0)

    def to_sibling(dx):
        remote(raw.at[0, dx], raw.at[1, dx], send_c.at[dx - 1], recv_c.at[dx - 1], sibling)

    def from_sibling(dx):
        take(raw.at[1, dx], recv_c.at[dx - 1])
        normalise(1, dx)

    def rows_of(dx):
        return pl.ds(pl.multiple_of(((x + dx) % NX) * BLOCK, 32), BLOCK)

    def project_kv(dx):
        product = dot(normed[rows_of(dx), :], wts[0], ((1,), (0,)))
        if dx == 0:
            own_kv[...] = product
        else:
            out_kv[dx - 1] = product.astype(BF16)
            remote(out_kv.at[dx - 1], in_kv.at[dx - 1], send_kv.at[dx - 1], recv_kv.at[dx - 1], chip(dx))

    def project_q(head, dx):
        piece = wts[1 + head // 2, :, (head % 2) * HD : (head % 2 + 1) * HD]
        product = dot(normed[rows_of(dx), :], piece, ((1,), (0,)))
        if dx == 0:
            own_q[head] = product
        else:
            out_q[head, dx - 1] = product.astype(BF16)
            remote(
                out_q.at[head, dx - 1],
                in_q.at[head, dx - 1],
                send_q.at[head, dx - 1],
                recv_q.at[head, dx - 1],
                chip(dx),
            )

    def query(head):
        for dx in range(3):
            take(in_q.at[head, dx], recv_q.at[head, dx])
        summed = own_q[head]
        for dx in range(3):
            summed = summed + in_q[head, dx].astype(F32)
        queries[head] = rotated(summed)

    def project(head, order=(2, 1, 3, 0)):
        for dx in order:
            if head is None:
                project_kv(dx)
            else:
                project_q(head, dx)

    def key_value():
        for dx in range(3):
            take(in_kv.at[dx], recv_kv.at[dx])
        keyvalue = own_kv[...]
        for dx in range(3):
            keyvalue = keyvalue + in_kv[dx].astype(F32)
        window[pl.ds(2 * BLOCK, BLOCK), 0:HD] = rotated(keyvalue[:, 0:HD])
        window[pl.ds(2 * BLOCK, BLOCK), HD : 2 * HD] = keyvalue[:, HD : 2 * HD].astype(BF16)
        next_block = at(s, 2 * micro + 1 - half, (y + half) % NY, z)
        for i, device in ((0, chip(0, 1)), (1, next_block)):
            remote(
                window.at[pl.ds(2 * BLOCK, BLOCK)],
                window.at[pl.ds(i * BLOCK, BLOCK)],
                send_h.at[i],
                recv_h.at[i],
                device,
            )

    take(raw.at[0, 0], sem_loc.at[5])
    take(raw.at[1, 0], sem_loc.at[6])
    for i in range(1, 3):
        take(wts.at[i, pl.ds(0, PIECE)], sem_loc.at[7 + i])
    ring(0, 2)
    normalise(0, 0)
    ring(1, 2)
    normalise(1, 0)
    ring(2, 2)
    ring(0, 3)
    ring_send(3, 1)
    ring(1, 3)
    ring_send(4, 1)
    ring(2, 3)
    for n, (dz, i) in enumerate(spread):
        take(quarters(quarter - dz, i), recv_z.at[n])
    to_sibling(2)
    normalise(0, 2)
    ring(3, 1)
    ring_send(5, 1)
    from_sibling(2)
    for d, dx in ((0, 3), (1, 1)):
        take(raw.at[0, dx], recv_a.at[d])
        to_sibling(dx)
    ring(4, 1)
    normalise(0, 3)
    normalise(0, 1)
    from_sibling(3)
    from_sibling(1)
    ring_take(0, 4)
    ring_take(1, 4)
    ring(3, 2)
    project(None, (2, 1))
    ring(5, 1)
    project(None, (3, 0))
    ring(4, 2)
    ring_take(2, 4)
    project(0)
    ring(3, 3)
    ring(5, 2)
    ring(4, 3)
    key_value()
    ring_take(3, 4)
    project(1)
    ring(5, 3)
    ring_take(4, 4)
    project(2)
    query(0)
    ring_take(5, 4)
    project(3)
    query(1)
    for i in range(2):
        take(window.at[pl.ds(i * BLOCK, BLOCK)], recv_h.at[i])

    key_row = (y * GROUP + half * BLOCK - GROUP + iota((1, WINDOW), 1)).astype(F32)

    def attend(head):
        logits = dot(queries[head], window[:, 0:HD], ((1,), (1,))) * SCALE
        allowed = (key_row >= opening) & (key_row <= row)
        weight = jnp.where(allowed, jnp.exp(logits), 0.0)
        probs = (weight / jnp.sum(weight, axis=1, keepdims=True)).astype(BF16)
        attended[pl.ds(0, BLOCK), :] = dot(probs, window[:, HD : 2 * HD], ((1,), (0,)))
        product = dot(heads[:, head * HD : (head + 1) * HD], attended[...], ((1,), (1,)), HIGHEST)
        if head == 0:
            part[...] = product
        else:
            part[...] += product

    attend(0)
    attend(1)
    query(2)
    attend(2)

    query(3)
    attend(3)

    rows = [part[k : k + 1, i * HD : (i + 1) * HD] for k in range(2) for i in range(3)]
    tile[...] = jnp.concatenate(rows + [jnp.zeros((2, HD), F32)], axis=0)
    for dz in range(1, NZ):
        remote(tile, terms.at[dz - 1], send_t, recv_t, over_z(dz))
    take(terms, recv_t)
    total = tile[...]
    for i in range(NZ - 1):
        total = total + terms[i]

    value, reward = chain(total[0:3]), chain(total[3:6])
    after = pltpu.roll(value, LANES - 1, 1)
    run = jnp.where(closing == now + 1.0, reward, 0.0) + jnp.where(now + 1.0 < limit, after, 0.0) - value
    for j in range(9):
        step = 2**j
        after = pltpu.roll(run, LANES - step, 1)
        run = run + jnp.where(now + step < limit, LAMBDA_GAE**step * after, 0.0)
    scanned = [total[0:3]] + [run[:, i * HD : (i + 1) * HD] for i in range(3)]
    scanned = jnp.concatenate(scanned + [jnp.zeros((2, HD), F32)], axis=0)
    results[...] = jnp.where(s == 0, total, scanned)

    def deliver(target, core, xc, yc, sem, recv, may_stay):
        if may_stay:
            here = (xc == x) & (yc == y)

            @pl.when(here)
            def _():
                local(results, target, recv)

            @pl.when(jnp.logical_not(here))
            def _():
                remote(results, target, sem, recv, at(core, xc, yc, z))

        else:
            remote(results, target, sem, recv, at(core, xc, yc, z))

    def settle(xc, yc, sem, may_stay):
        if may_stay:

            @pl.when(jnp.logical_not((xc == x) & (yc == y)))
            def _():
                take(results, sem)

        else:
            take(results, sem)

    @pl.when(s == 0)
    def _():
        for i in range(4):
            core, xc = i // 2, 2 * half + i % 2
            deliver(scores.at[micro], core, xc, y, send_g.at[i], recv_p.at[micro], core == 0)

    @pl.when(s == 1)
    def _():
        for k in range(3):
            index = 2 * y + half - k + 2 * NY
            for i in range(4):
                core, xc, yc = i // 2, 2 * (index % 2) + i % 2, (index // 2) % NY
                deliver(
                    blocks.at[micro, k], core, xc, yc, send_g.at[4 * k + i], recv_g.at[micro, k], k < 2 and core == 1
                )

    def outgoing(line):
        return jnp.where(half == 0, line[:, 0:ROWS], line[:, ROWS : 2 * ROWS])

    for m in range(2):
        take(scores.at[m], recv_p.at[m])
        for k in range(3):
            take(blocks.at[m, k], recv_g.at[m, k])
        decay, through = carries[m]
        third = blocks[m, 2, 0:1, 0:1] + LAMBDA_GAE * blocks[m, 2, 3:4, 0:1]
        following = blocks[m, 1, 3:4, 0:1] + through * third
        carry = blocks[m, 1, 0:1, 0:1] + LAMBDA_GAE * following
        value = chain(blocks[m, 0, 0:3])
        advantage = chain(blocks[m, 0, 3:6]) + decay * carry
        out[m : m + 1, :] = outgoing(chain(scores[m, 0:3]))
        out[2 + m : 3 + m, :] = outgoing(advantage)
        out[4 + m : 5 + m, :] = outgoing(advantage + value)

    take(quarters(quarter), send_d)
    for d, dx in ((0, 1), (1, NX - 1)):
        take(raw.at[0, NX - dx], send_a.at[d])
    take(scales.at[pl.ds(1, 7)], send_s)
    for n, (dz, i) in enumerate(spread):
        take(quarters(quarter, i), send_z.at[n])
    for p in range(PIECES):
        for step in range(1, 5):
            ring_take(p, step, send_b)
    for dx in range(3):
        take(raw.at[1, dx + 1], send_c.at[dx])
        take(out_kv.at[dx], send_kv.at[dx])
        for head in range(4):
            take(out_q.at[head, dx], send_q.at[head, dx])
    for i in range(2):
        take(window.at[pl.ds(i * BLOCK, BLOCK)], send_h.at[i])
    take(terms, send_t)

    @pl.when(s == 0)
    def _():
        for i in range(4):
            settle(2 * half + i % 2, y, send_g.at[i], i // 2 == 0)

    @pl.when(s == 1)
    def _():
        for k in range(3):
            index = 2 * y + half - k + 2 * NY
            for i in range(4):
                settle(2 * (index % 2) + i % 2, (index // 2) % NY, send_g.at[4 * k + i], k < 2 and i // 2 == 1)


def split_kernel(lines, scores_out, adv_out, ret_out):
    scores_out[...] = lines[0:2]
    adv_out[...] = lines[2:4]
    ret_out[...] = lines[4:6]


def on_device(hidden, norm_gain, query_weight, keyvalue_weight, policy_head, critic_heads, lengths):
    hbm = pl.BlockSpec(memory_space=pl.ANY)
    dma = pltpu.SemaphoreType.DMA
    vmem = pltpu.VMEM
    lines = pl.pallas_call(
        section_kernel,
        out_shape=jax.ShapeDtypeStruct((8, ROWS), F32),
        in_specs=[hbm] * 7,
        out_specs=pl.BlockSpec(memory_space=pltpu.VMEM),
        scratch_shapes=[
            vmem((ROWS, WIDTH), BF16),
            vmem((2, NX, NY, ROWS, PIECE), BF16),
            vmem((2 * GROUP, NY * PIECE), BF16),
            vmem((2 * PIECE, HD), BF16),
            vmem((3, NY * PIECE, PIECE), BF16),
            vmem((8, 8, ROWS), F32),
            vmem((1, WIDTH), F32),
            vmem((1, 4 * HD), F32),
            vmem((2, 4 * HD), F32),
            vmem((2, NRESP), jnp.int32),
            vmem((BLOCK, PIECE), F32),
            vmem((4, BLOCK, HD), F32),
            vmem((3, BLOCK, PIECE), BF16),
            vmem((3, BLOCK, PIECE), BF16),
            vmem((4, 3, BLOCK, HD), BF16),
            vmem((4, 3, BLOCK, HD), BF16),
            vmem((4, BLOCK, HD), BF16),
            vmem((WINDOW, PIECE), BF16),
            vmem((LANES, HD), F32),
            vmem((8, LANES), F32),
            vmem((8, HD), F32),
            vmem((NZ - 1, 8, HD), F32),
            vmem((8, HD), F32),
            vmem((2, 3, 8, HD), F32),
            vmem((2, 8, HD), F32),
            dma((10,)), dma((2,)), dma((2,)), dma, dma, dma((4,)), dma((4,)), dma((3,)), dma((3,)), dma, dma,
            dma((PIECES, 4, 2)), dma((PIECES, 4, 2)), dma((3,)), dma((3,)), dma((4, 3)), dma((4, 3)),
            dma((2,)), dma((2,)), dma, dma, dma((12,)), dma((2, 3)), dma((2,)),
        ],
        compiler_params=pltpu.CompilerParams(
            collective_id=0, has_side_effects=True, vmem_limit_bytes=60 * 1024 * 1024
        ),
        name="section",
    )(
        hidden,
        norm_gain,
        query_weight[0],
        keyvalue_weight.reshape(2 * PIECE, HD),
        policy_head.reshape(1, -1),
        critic_heads,
        lengths,
    )
    line = jax.ShapeDtypeStruct((2, ROWS), F32)
    return pl.pallas_call(split_kernel, out_shape=(line, line, line), name="split")(lines)


def solution(mesh):
    placed = (
        P(None, "seq", None),
        P("sec", None),
        P("sec", "seq", "mp"),
        P("sec", "seq", None, "mp"),
        P("mp"),
        P(None, "mp"),
        P(),
    )
    return jax.shard_map(
        on_device,
        mesh=mesh,
        in_specs=placed,
        out_specs=(P(None, "seq"), P(None, "seq"), P(None, "seq")),
        check_vma=False,
    )
```

```python
import functools

import jax
import jax.numpy as jnp
from jax import lax
from jax.experimental import pallas as pl
from jax.experimental.pallas import tpu as pltpu
from jax.sharding import PartitionSpec as P

F32 = jnp.float32
BF16 = jnp.bfloat16
MESH = pl.DeviceIdType.MESH
HIGHEST = lax.Precision.HIGHEST

HD = 128
NX, NY, NZ = 4, 8, 8
ROWS = 144
BLOCK = 288
GROUP = 576
WINDOW = 864
WIDTH = 8192
PIECE = 256
NRESP = 64
LANES = 384
PIECES = 6
LAMBDA_GAE = 0.95
LOG_LAMBDA = -0.05129329438755058
LOG_BASE = 13.815510557964274
NORM_EPS = 1e-06
SCALE = float(HD) ** -0.5

REL = (0, 1, -1, 2, -2, 3, -3, 4)
PLACE = {0: 0, 1: 1, -1: 2, 2: 3, -2: 4, 3: 5, -3: 6, 4: 7, -4: 7}


def rel_of(place):
    return ((place + 1) // 2) * (2 * (place % 2) - 1)


def remote(src, dst, send, recv, device):
    copy = pltpu.make_async_remote_copy(
        src_ref=src, dst_ref=dst, send_sem=send, recv_sem=recv, device_id=device, device_id_type=MESH
    )
    copy.start()


def local(src, dst, sem):
    pltpu.make_async_copy(src, dst, sem).start()


def take(ref, sem):
    pltpu.make_async_copy(ref, ref, sem).wait()


def iota(shape, axis):
    return lax.broadcasted_iota(jnp.int32, shape, axis)


def dot(a, b, over, precision=None):
    return lax.dot_general(
        a, b, ((over[0], over[1]), ((), ())), precision=precision, preferred_element_type=F32
    )


def chain(refs):
    return jnp.concatenate([refs[i : i + 1] for i in range(3)], axis=1)


def closing_row(lengths):
    upto = (iota((NRESP, NRESP), 0) <= iota((NRESP, NRESP), 1)).astype(F32)
    return dot(lengths, upto, ((1,), (0,)), HIGHEST)


def closing_column(lengths):
    upto = (iota((NRESP, NRESP), 1) <= iota((NRESP, NRESP), 0)).astype(F32)
    return dot(upto, lengths, ((1,), (1,)), HIGHEST)


def places():
    s = lax.axis_index("sec")
    q = lax.axis_index("seq")
    z = lax.axis_index("mp")
    return s, q % NX, q // NX, z


def at(s, x, y, z):
    return (s, y * NX + x, z)


def section_kernel(
    hid, gain_hbm, qw, kvw, policy_hbm, critic_hbm, lengths_hbm, out,
    hbuf, raw, normed, pairs, wts, scales, gain, policy, critic, lengths,
    own_kv, own_q, out_kv, in_kv, out_q, in_q, queries, window, attended, part, tile, terms, results, blocks, scores,
    sem_loc, send_a, recv_a, send_d, recv_d, send_z, recv_z, send_c, recv_c, send_s, recv_s, send_b, recv_b,
    send_kv, recv_kv, send_q, recv_q, send_h, recv_h, send_t, recv_t, send_g, recv_g, recv_p,
):
    s, x, y, z = places()
    micro, half = x // 2, x % 2
    other = 1 - s

    def chip(dx=0, dy=0, core=None):
        return at(s if core is None else core, (x + dx) % NX, (y + dy + NY) % NY, z)

    def over_z(dz):
        return at(s, x, y, (z + dz + NZ) % NZ)

    sibling = at(other, x, y, z)
    barrier = pltpu.get_barrier_semaphore()
    partners = [chip(dx, 0, (s + ds) % 2) for ds in range(2) for dx in range(NX)][1:]
    partners = partners + [chip(dx, dy, core) for core in range(2) for dx in range(NX) for dy in (-1, 1)]
    partners = partners + [over_z(dz) for dz in range(1, NZ)]
    for device in partners:
        pl.semaphore_signal(barrier, inc=1, device_id=device, device_id_type=MESH)
    def column(place, xx):
        start = ((y + rel_of(place) + NY) % NY) * (NX * PIECE) + xx * PIECE
        return pl.ds(pl.multiple_of(start, PIECE), PIECE)

    local(hid.at[s], hbuf, sem_loc.at[0])
    local(kvw, pairs, sem_loc.at[7])
    local(gain_hbm, gain, sem_loc.at[1])
    local(policy_hbm, policy, sem_loc.at[2])
    local(critic_hbm, critic, sem_loc.at[3])
    local(lengths_hbm, lengths, sem_loc.at[4])
    for place in range(NY):
        local(hid.at[s, :, column(place, x)], raw.at[0, 0, place], sem_loc.at[5])
        local(hid.at[other, :, column(place, x)], raw.at[1, 0, place], sem_loc.at[6])
    for i in range(2):
        local(qw.at[:, pl.ds(i * PIECE, PIECE)], wts.at[i + 1, pl.ds(0, PIECE)], sem_loc.at[8 + i])

    take(hbuf, sem_loc.at[0])

    def squares(i, total):
        for j in range(4):
            start = pl.multiple_of((i * 4 + j) * HD, HD)
            block = hbuf[:, pl.ds(start, HD)].astype(F32)
            total = total + block * block
        return total

    total = lax.fori_loop(0, WIDTH // HD // 4, squares, jnp.zeros((ROWS, HD), F32))
    mean = dot(jnp.ones((8, HD), F32), total, ((1,), (1,)), HIGHEST) * (1.0 / WIDTH)
    scales[0] = lax.rsqrt(mean + NORM_EPS)
    take(pairs, sem_loc.at[7])
    for i in range(2):
        chosen = iota((PIECE, 2 * PIECE), 1) == 2 * iota((PIECE, 2 * PIECE), 0) + i
        sorted_rows = dot(chosen.astype(F32).astype(BF16), pairs[...], ((1,), (0,)))
        wts[0, 0:PIECE, i * HD : (i + 1) * HD] = sorted_rows.astype(BF16)

    pl.semaphore_wait(barrier, len(partners))

    def weights(p, place, piece=None):
        begin, size = place * PIECE, PIECE
        if piece is not None:
            begin, size = begin + piece * (PIECE // 2), PIECE // 2
        return wts.at[p // 2, pl.ds(begin, size), pl.ds((p % 2) * HD, HD)]

    def mine(p):
        return weights(p, 0) if p < 2 else qw.at[:, pl.ds((p - 2) * HD, HD)]

    ring_y = [chip(0, 1), chip(0, -1)]

    def ring_send(p, step, ways=(0, 1)):
        for d in ways:
            sign, piece = 1 - 2 * d, d if step == 4 else None
            target = weights(p, PLACE[-sign * step], piece)
            source = mine(p) if step == 1 else weights(p, PLACE[-sign * (step - 1)], piece)
            remote(source, target, send_b.at[p, step - 1, d], recv_b.at[p, step - 1, d], ring_y[d])

    def ring_take(p, step, sems=None, ways=(0, 1)):
        sems = recv_b if sems is None else sems
        for d in ways:
            sign, piece = 1 - 2 * d, d if step == 4 else None
            take(weights(p, PLACE[-sign * step], piece), sems.at[p, step - 1, d])

    def ring(p, step):
        for d in range(2):
            ring_take(p, step, None, (d,))
            ring_send(p, step + 1, (d,))

    def to_neighbours(place):
        for d, dx in ((0, 1), (1, NX - 1)):
            remote(
                hid.at[s, :, column(place, (x + dx) % NX)],
                raw.at[0, NX - dx, place],
                send_a.at[d],
                recv_a.at[d],
                chip(dx),
            )

    for p in range(3):
        ring_send(p, 1)
    facing = (x + 2) % NX
    quarter = z % 4
    for i in range(2):
        remote(
            hid.at[s, :, column(2 * quarter + i, facing)], raw.at[0, 2, 2 * quarter + i], send_d, recv_d, chip(2)
        )
    for ds in range(2):
        for dx in range(NX):
            if ds + dx > 0:
                slot = ((2 - ds) % 2) * NX + (NX - dx) % NX
                remote(scales.at[0], scales.at[slot], send_s, recv_s, chip(dx, 0, (s + ds) % 2))
    def quarters(t, i=None):
        begin = 2 * ((t + 4) % 4)
        return raw.at[0, 2, pl.ds(begin, 2)] if i is None else raw.at[0, 2, begin + i]

    spread = ((1, None), (-1, None), (2, 1), (-2, 0))
    for place in range(NY):
        to_neighbours(place)

    ring(0, 1)
    ring(1, 1)
    take(quarters(quarter), recv_d)
    for n, (dz, i) in enumerate(spread):
        remote(quarters(quarter, i), quarters(quarter, i), send_z.at[n], recv_z.at[n], over_z(dz))
    ring(2, 1)

    take(lengths, sem_loc.at[4])
    lens = lengths[...].astype(F32)
    openings = closing_row(lens) - lens
    opening_line = jnp.where(micro == 0, openings[0:1], openings[1:2])
    row = (y * GROUP + half * BLOCK + iota((BLOCK, 1), 0)).astype(F32)
    opening = jnp.max(jnp.where(opening_line <= row, opening_line, 0.0), axis=1, keepdims=True)
    lane = iota((1, HD), 1)
    inverse = jnp.exp((lane % (HD // 2)).astype(F32) * (-2.0 * LOG_BASE / HD))
    angle = (row - opening) * inverse
    cosine = jnp.cos(angle)
    sine = jnp.sin(angle) * jnp.where(lane < HD // 2, -1.0, 1.0)

    def rotated(v):
        return (v * cosine + pltpu.roll(v, HD // 2, 1) * sine).astype(BF16)

    ends = closing_column(lens)

    def end_of(line, base):
        now = (base + iota((1, LANES), 1)).astype(F32)
        return now, jnp.min(jnp.where(line > now, line, 1e9), axis=0, keepdims=True)

    begin = y * GROUP + half * BLOCK
    now, closing = end_of(jnp.where(micro == 0, ends[:, 0:1], ends[:, 1:2]), begin)
    limit = jnp.minimum(closing, (begin + BLOCK).astype(F32))
    given = y * GROUP + (x // 2) * BLOCK
    carries = []
    for m in range(2):
        there, finish = end_of(ends[:, m : m + 1], given)
        edge = (given + BLOCK).astype(F32)
        decay = jnp.exp(jnp.maximum(edge - 1.0 - there, 0.0) * LOG_LAMBDA)
        decay = jnp.where((finish > edge) & (there < edge), decay, 0.0)
        line = ends[:, m : m + 1]
        beyond = jnp.min(jnp.where(line > edge, line, 1e9), axis=0, keepdims=True)
        through = jnp.where(beyond > edge + BLOCK, LAMBDA_GAE ** (BLOCK - 1), 0.0)
        carries.append((decay, through))

    take(policy, sem_loc.at[2])
    take(critic, sem_loc.at[3])
    kind = iota((8, 4 * HD), 0)
    first = jnp.where(s == 0, policy[...], critic[0:1])
    second = jnp.where(s == 0, 0.0, critic[1:2])
    heads = jnp.where(kind == 0, first, jnp.where(kind == 1, second, 0.0))
    attended[pl.ds(BLOCK, LANES - BLOCK), :] = jnp.zeros((LANES - BLOCK, HD), F32)

    take(scales.at[pl.ds(1, 7)], recv_s)
    take(gain, sem_loc.at[1])

    def normalise(ds, dx):
        base = (((s + ds) % 2) * NX + (x + dx) % NX) * ROWS
        rows = pl.ds(pl.multiple_of(base, 16), ROWS)
        first_row = (iota((8, PIECE), 0) == 0).astype(F32)
        scale = dot(scales[ds * NX + dx], first_row, ((0,), (0,)), HIGHEST)

        def one(place, carry):
            block = raw[ds, dx, place].astype(F32) * scale * gain[0:1, column(place, x)]
            normed[rows, pl.ds(pl.multiple_of(place * PIECE, PIECE), PIECE)] = block.astype(BF16)
            return carry

        lax.fori_loop(0, NY, one, 0)

    def to_sibling(dx):
        remote(raw.at[0, dx], raw.at[1, dx], send_c.at[dx - 1], recv_c.at[dx - 1], sibling)

    def from_sibling(dx):
        take(raw.at[1, dx], recv_c.at[dx - 1])
        normalise(1, dx)

    def rows_of(dx):
        return pl.ds(pl.multiple_of(((x + dx) % NX) * BLOCK, 32), BLOCK)

    def project_kv(dx):
        product = dot(normed[rows_of(dx), :], wts[0], ((1,), (0,)))
        if dx == 0:
            own_kv[...] = product
        else:
            out_kv[dx - 1] = product.astype(BF16)
            remote(out_kv.at[dx - 1], in_kv.at[dx - 1], send_kv.at[dx - 1], recv_kv.at[dx - 1], chip(dx))

    def project_q(head, dx):
        piece = wts[1 + head // 2, :, (head % 2) * HD : (head % 2 + 1) * HD]
        product = dot(normed[rows_of(dx), :], piece, ((1,), (0,)))
        if dx == 0:
            own_q[head] = product
        else:
            out_q[head, dx - 1] = product.astype(BF16)
            remote(
                out_q.at[head, dx - 1],
                in_q.at[head, dx - 1],
                send_q.at[head, dx - 1],
                recv_q.at[head, dx - 1],
                chip(dx),
            )

    def query(head):
        for dx in range(3):
            take(in_q.at[head, dx], recv_q.at[head, dx])
        summed = own_q[head]
        for dx in range(3):
            summed = summed + in_q[head, dx].astype(F32)
        queries[head] = rotated(summed)

    def project(head, order=(2, 1, 3, 0)):
        for dx in order:
            if head is None:
                project_kv(dx)
            else:
                project_q(head, dx)

    def key_value():
        for dx in range(3):
            take(in_kv.at[dx], recv_kv.at[dx])
        keyvalue = own_kv[...]
        for dx in range(3):
            keyvalue = keyvalue + in_kv[dx].astype(F32)
        window[pl.ds(2 * BLOCK, BLOCK), 0:HD] = rotated(keyvalue[:, 0:HD])
        window[pl.ds(2 * BLOCK, BLOCK), HD : 2 * HD] = keyvalue[:, HD : 2 * HD].astype(BF16)
        next_block = at(s, 2 * micro + 1 - half, (y + half) % NY, z)
        for i, device in ((0, chip(0, 1)), (1, next_block)):
            remote(
                window.at[pl.ds(2 * BLOCK, BLOCK)],
                window.at[pl.ds(i * BLOCK, BLOCK)],
                send_h.at[i],
                recv_h.at[i],
                device,
            )

    take(raw.at[0, 0], sem_loc.at[5])
    take(raw.at[1, 0], sem_loc.at[6])
    for i in range(1, 3):
        take(wts.at[i, pl.ds(0, PIECE)], sem_loc.at[7 + i])
    ring(0, 2)
    normalise(0, 0)
    ring(1, 2)
    normalise(1, 0)
    ring(2, 2)
    ring(0, 3)
    ring_send(3, 1)
    ring(1, 3)
    ring_send(4, 1)
    ring(2, 3)
    for n, (dz, i) in enumerate(spread):
        take(quarters(quarter - dz, i), recv_z.at[n])
    to_sibling(2)
    normalise(0, 2)
    ring(3, 1)
    ring_send(5, 1)
    from_sibling(2)
    for d, dx in ((0, 3), (1, 1)):
        take(raw.at[0, dx], recv_a.at[d])
        to_sibling(dx)
    ring(4, 1)
    normalise(0, 3)
    normalise(0, 1)
    from_sibling(3)
    from_sibling(1)
    ring_take(0, 4)
    ring_take(1, 4)
    ring(3, 2)
    project(None, (2, 1))
    ring(5, 1)
    project(None, (3, 0))
    ring(4, 2)
    ring_take(2, 4)
    project(0)
    ring(3, 3)
    ring(5, 2)
    ring(4, 3)
    key_value()
    ring_take(3, 4)
    project(1)
    ring(5, 3)
    ring_take(4, 4)
    project(2)
    query(0)
    ring_take(5, 4)
    project(3)
    query(1)
    for i in range(2):
        take(window.at[pl.ds(i * BLOCK, BLOCK)], recv_h.at[i])

    key_row = (y * GROUP + half * BLOCK - GROUP + iota((1, WINDOW), 1)).astype(F32)

    def attend(head):
        logits = dot(queries[head], window[:, 0:HD], ((1,), (1,))) * SCALE
        allowed = (key_row >= opening) & (key_row <= row)
        weight = jnp.where(allowed, jnp.exp(logits), 0.0)
        probs = (weight / jnp.sum(weight, axis=1, keepdims=True)).astype(BF16)
        attended[pl.ds(0, BLOCK), :] = dot(probs, window[:, HD : 2 * HD], ((1,), (0,)))
        product = dot(heads[:, head * HD : (head + 1) * HD], attended[...], ((1,), (1,)), HIGHEST)
        if head == 0:
            part[...] = product
        else:
            part[...] += product

    attend(0)
    attend(1)
    query(2)
    attend(2)

    query(3)
    attend(3)

    rows = [part[k : k + 1, i * HD : (i + 1) * HD] for k in range(2) for i in range(3)]
    tile[...] = jnp.concatenate(rows + [jnp.zeros((2, HD), F32)], axis=0)
    for dz in range(1, NZ):
        remote(tile, terms.at[dz - 1], send_t, recv_t, over_z(dz))

    take(quarters(quarter), send_d)
    for d, dx in ((0, 1), (1, NX - 1)):
        take(raw.at[0, NX - dx], send_a.at[d])
    take(scales.at[pl.ds(1, 7)], send_s)
    for n, (dz, i) in enumerate(spread):
        take(quarters(quarter, i), send_z.at[n])
    for p in range(PIECES):
        for step in range(1, 5):
            ring_take(p, step, send_b)
    for dx in range(3):
        take(raw.at[1, dx + 1], send_c.at[dx])
        take(out_kv.at[dx], send_kv.at[dx])
        for head in range(4):
            take(out_q.at[head, dx], send_q.at[head, dx])
    for i in range(2):
        take(window.at[pl.ds(i * BLOCK, BLOCK)], send_h.at[i])

    take(terms, recv_t)
    total = tile[...]
    for i in range(NZ - 1):
        total = total + terms[i]

    value, reward = chain(total[0:3]), chain(total[3:6])
    after = pltpu.roll(value, LANES - 1, 1)
    run = jnp.where(closing == now + 1.0, reward, 0.0) + jnp.where(now + 1.0 < limit, after, 0.0) - value
    for j in range(9):
        step = 2**j
        after = pltpu.roll(run, LANES - step, 1)
        run = run + jnp.where(now + step < limit, LAMBDA_GAE**step * after, 0.0)
    scanned = [total[0:3]] + [run[:, i * HD : (i + 1) * HD] for i in range(3)]
    scanned = jnp.concatenate(scanned + [jnp.zeros((2, HD), F32)], axis=0)
    results[...] = jnp.where(s == 0, total, scanned)

    def deliver(target, core, xc, yc, sem, recv, may_stay):
        if may_stay:
            here = (xc == x) & (yc == y)

            @pl.when(here)
            def _():
                local(results, target, recv)

            @pl.when(jnp.logical_not(here))
            def _():
                remote(results, target, sem, recv, at(core, xc, yc, z))

        else:
            remote(results, target, sem, recv, at(core, xc, yc, z))

    def settle(xc, yc, sem, may_stay):
        if may_stay:

            @pl.when(jnp.logical_not((xc == x) & (yc == y)))
            def _():
                take(results, sem)

        else:
            take(results, sem)

    @pl.when(s == 0)
    def _():
        for i in range(4):
            core, xc = i // 2, 2 * half + i % 2
            deliver(scores.at[micro], core, xc, y, send_g.at[i], recv_p.at[micro], core == 0)

    @pl.when(s == 1)
    def _():
        for k in range(3):
            index = 2 * y + half - k + 2 * NY
            for i in range(4):
                core, xc, yc = i // 2, 2 * (index % 2) + i % 2, (index // 2) % NY
                deliver(
                    blocks.at[micro, k], core, xc, yc, send_g.at[4 * k + i], recv_g.at[micro, k], k < 2 and core == 1
                )

    def outgoing(line):
        return jnp.where(half == 0, line[:, 0:ROWS], line[:, ROWS : 2 * ROWS])

    for m in range(2):
        take(scores.at[m], recv_p.at[m])
        for k in range(3):
            take(blocks.at[m, k], recv_g.at[m, k])
        decay, through = carries[m]
        third = blocks[m, 2, 0:1, 0:1] + LAMBDA_GAE * blocks[m, 2, 3:4, 0:1]
        following = blocks[m, 1, 3:4, 0:1] + through * third
        carry = blocks[m, 1, 0:1, 0:1] + LAMBDA_GAE * following
        value = chain(blocks[m, 0, 0:3])
        advantage = chain(blocks[m, 0, 3:6]) + decay * carry
        out[m : m + 1, :] = outgoing(chain(scores[m, 0:3]))
        out[2 + m : 3 + m, :] = outgoing(advantage)
        out[4 + m : 5 + m, :] = outgoing(advantage + value)

    take(terms, send_t)

    @pl.when(s == 0)
    def _():
        for i in range(4):
            settle(2 * half + i % 2, y, send_g.at[i], i // 2 == 0)

    @pl.when(s == 1)
    def _():
        for k in range(3):
            index = 2 * y + half - k + 2 * NY
            for i in range(4):
                settle(2 * (index % 2) + i % 2, (index // 2) % NY, send_g.at[4 * k + i], k < 2 and i // 2 == 1)


def split_kernel(lines, scores_out, adv_out, ret_out):
    scores_out[...] = lines[0:2]
    adv_out[...] = lines[2:4]
    ret_out[...] = lines[4:6]


def on_device(hidden, norm_gain, query_weight, keyvalue_weight, policy_head, critic_heads, lengths):
    hbm = pl.BlockSpec(memory_space=pl.ANY)
    dma = pltpu.SemaphoreType.DMA
    vmem = pltpu.VMEM
    lines = pl.pallas_call(
        section_kernel,
        out_shape=jax.ShapeDtypeStruct((8, ROWS), F32),
        in_specs=[hbm] * 7,
        out_specs=pl.BlockSpec(memory_space=pltpu.VMEM),
        scratch_shapes=[
            vmem((ROWS, WIDTH), BF16),
            vmem((2, NX, NY, ROWS, PIECE), BF16),
            vmem((2 * GROUP, NY * PIECE), BF16),
            vmem((2 * PIECE, HD), BF16),
            vmem((3, NY * PIECE, PIECE), BF16),
            vmem((8, 8, ROWS), F32),
            vmem((1, WIDTH), F32),
            vmem((1, 4 * HD), F32),
            vmem((2, 4 * HD), F32),
            vmem((2, NRESP), jnp.int32),
            vmem((BLOCK, PIECE), F32),
            vmem((4, BLOCK, HD), F32),
            vmem((3, BLOCK, PIECE), BF16),
            vmem((3, BLOCK, PIECE), BF16),
            vmem((4, 3, BLOCK, HD), BF16),
            vmem((4, 3, BLOCK, HD), BF16),
            vmem((4, BLOCK, HD), BF16),
            vmem((WINDOW, PIECE), BF16),
            vmem((LANES, HD), F32),
            vmem((8, LANES), F32),
            vmem((8, HD), F32),
            vmem((NZ - 1, 8, HD), F32),
            vmem((8, HD), F32),
            vmem((2, 3, 8, HD), F32),
            vmem((2, 8, HD), F32),
            dma((10,)), dma((2,)), dma((2,)), dma, dma, dma((4,)), dma((4,)), dma((3,)), dma((3,)), dma, dma,
            dma((PIECES, 4, 2)), dma((PIECES, 4, 2)), dma((3,)), dma((3,)), dma((4, 3)), dma((4, 3)),
            dma((2,)), dma((2,)), dma, dma, dma((12,)), dma((2, 3)), dma((2,)),
        ],
        compiler_params=pltpu.CompilerParams(
            collective_id=0, has_side_effects=True, vmem_limit_bytes=60 * 1024 * 1024
        ),
        name="section",
    )(
        hidden,
        norm_gain,
        query_weight[0],
        keyvalue_weight.reshape(2 * PIECE, HD),
        policy_head.reshape(1, -1),
        critic_heads,
        lengths,
    )
    line = jax.ShapeDtypeStruct((2, ROWS), F32)
    return pl.pallas_call(split_kernel, out_shape=(line, line, line), name="split")(lines)


def solution(mesh):
    placed = (
        P(None, "seq", None),
        P("sec", None),
        P("sec", "seq", "mp"),
        P("sec", "seq", None, "mp"),
        P("mp"),
        P(None, "mp"),
        P(),
    )
    return jax.shard_map(
        on_device,
        mesh=mesh,
        in_specs=placed,
        out_specs=(P(None, "seq"), P(None, "seq"), P(None, "seq")),
        check_vma=False,
    )
```
